256 devices in a mesh: gx: 8 (over x, core), gy: 32 (over z, y).
Axes of the slice: x: 4, y: 4, z: 8, core: 2. Of those that a mesh axis runs over, the one named last changes fastest.
Arguments:
- prompt_tokens: bfloat16 [512, 18432], P(None, ('gx', 'gy')), may hold values from -6 to 6
- decode_tokens: bfloat16 [4, 128, 18432], P(None, None, ('gx', 'gy')), may hold values from -6 to 6
- gate_weight: bfloat16 [18432, 36864], P('gx', 'gy'), may hold values from -0.046875 to 0.046875
- up_weight: bfloat16 [18432, 36864], P('gx', 'gy'), may hold values from -0.046875 to 0.046875
Outputs:
- prompt_hidden: bfloat16 [512, 36864], P('gx', 'gy')
- decode_hidden: bfloat16 [4, 128, 36864], P(None, 'gx', 'gy')
The draws below stay inside these ranges and needn't reach their ends.
All inputs are finite; a program needn't handle non-finite values.
Results may differ from the reference program's by a relative error of at most 0.025.
Values may be sent and summed in bfloat16 or wider, within the bound.
A program may use at most 64 MiB of HBM per device.

```python
import jax
import jax.numpy as jnp
from jax import lax

D = 18432
FF = 36864
PROMPT = 512
BATCH = 128
STEPS = 4
N_GX = 8


def shard_levels(key, extent, pieces, smallest, top_value):
    gain, own = 1.0, jax.random.fold_in(key, 6)
    for position, parts in pieces:
        draws = jnp.exp(jax.random.uniform(jax.random.fold_in(own, position), (parts,), jnp.float32, smallest / len(pieces), top_value / len(pieces)))
        gain = gain * jnp.repeat(draws, extent[position] // parts).reshape([-1 if axis == position else 1 for axis in range(len(extent))])
    return gain


def centred(key, extent, deviation, limit, cuts=(), dtype=jnp.bfloat16):
    drawn = jax.random.normal(key, extent, jnp.float32) * deviation
    if len(cuts) > 0:
        drawn = shard_levels(key, extent, cuts, -0.22, 0.18) * drawn
    return jnp.clip(drawn, min=-limit, max=limit).astype(dtype)


def setup_inputs(seed: int = 0) -> dict:
    arg_keys = jax.random.split(jax.random.key(seed), 5)
    prompt_tokens = centred(arg_keys[0], (PROMPT, D), 1.0, 6.0, ((1, 256),))
    decode_tokens = centred(arg_keys[1], (STEPS, BATCH, D), 1.0, 6.0, ((2, 256),))
    gate_weight = centred(arg_keys[2], (D, FF), D ** -0.5, 0.046875, ((0, 8), (1, 32)))
    up_weight = centred(arg_keys[3], (D, FF), D ** -0.5, 0.046875, ((0, 8), (1, 32)))
    return {"prompt_tokens": prompt_tokens, "decode_tokens": decode_tokens, "gate_weight": gate_weight, "up_weight": up_weight}


def slab_sums(rows_in, gate_weight, up_weight):
    slab_width = D // N_GX
    gate_total = jnp.zeros((rows_in.shape[0], FF), jnp.float32)
    up_total = jnp.zeros((rows_in.shape[0], FF), jnp.float32)
    for slab in range(N_GX):
        begin_at = slab * slab_width
        end_at = begin_at + slab_width
        piece = rows_in[:, begin_at:end_at].astype(jnp.float32)
        gate_part = jnp.dot(piece, gate_weight[begin_at:end_at].astype(jnp.float32), precision=lax.Precision.HIGHEST)
        up_part = jnp.dot(piece, up_weight[begin_at:end_at].astype(jnp.float32), precision=lax.Precision.HIGHEST)
        gate_round = lax.optimization_barrier(gate_part.astype(jnp.bfloat16))
        up_round = lax.optimization_barrier(up_part.astype(jnp.bfloat16))
        gate_total = gate_total + gate_round.astype(jnp.float32)
        up_total = up_total + up_round.astype(jnp.float32)
    return (jax.nn.silu(gate_total) * up_total).astype(jnp.bfloat16)


def reference(prompt_tokens, decode_tokens, gate_weight, up_weight):
    prompt_hidden = slab_sums(prompt_tokens, gate_weight, up_weight)
    flat_rows = decode_tokens.reshape(STEPS * BATCH, D)
    decode_hidden = slab_sums(flat_rows, gate_weight, up_weight).reshape(STEPS, BATCH, FF)
    return prompt_hidden, decode_hidden
```

```python
import functools

import jax
import jax.numpy as jnp
from jax import lax
from jax.experimental import pallas as pl
from jax.experimental.pallas import tpu as pltpu
from jax.sharding import PartitionSpec as P

MESH = pl.DeviceIdType.MESH
NX, NZ, NY = 4, 8, 4
CHUNKS = 4
THIRDS = 3
GROUPS = CHUNKS * THIRDS
BF16, F32 = jnp.bfloat16, jnp.float32


def kernel(prompt, decode, gate, up, out_p, out_d, pieces, wbuf, xs, tails, own, psend, precv,
           s1_out, s1_in, s2_out, s2_in, ag_send, ag_recv, rs_send, rs_recv, w_sem):
    gx, gy = lax.axis_index("gx"), lax.axis_index("gy")
    x, core = gx // 2, gx % 2
    z, y = gy // NY, gy % NY

    def at_x(shift):
        return lax.rem(x + shift + NX, NX)

    def at_y(shift):
        return lax.rem(y + shift + NY, NY)

    def at_z(shift):
        return lax.rem(z + shift + NZ, NZ)

    other_core = {"gx": x * 2 + (1 - core), "gy": gy}
    x_up, x_down = ({"gx": at_x(s) * 2 + core, "gy": gy} for s in (1, -1))
    y_up, y_down = ({"gx": gx, "gy": z * NY + at_y(s)} for s in (1, -1))
    z_up, z_down = ({"gx": gx, "gy": at_z(s) * NY + y} for s in (1, -1))

    for j in range(9):
        for half, source in enumerate((gate, up)):
            for begin, rows, to in ((0, 64, 0), (80, 64, 64), (64, 16, 128)):
                pltpu.make_async_copy(
                    source.at[:, pl.ds(begin, rows), pl.ds(128 * j, 128)],
                    wbuf.at[j, :, pl.ds(to, rows), pl.ds(128 * half, 128)],
                    w_sem.at[j],
                ).start()

    barrier = pltpu.get_barrier_semaphore()
    for device in (other_core, x_up, x_down, y_up, y_down, z_up, z_down):
        pl.semaphore_signal(barrier, inc=1, device_id=device, device_id_type=MESH)

    odd = y % 2

    def picks(shape, row_of, col_of):
        r = lax.broadcasted_iota(jnp.int32, shape, 0)
        c = lax.broadcasted_iota(jnp.int32, shape, 1)
        return jnp.where(row_of(r, c) & col_of(r, c), 1.0, 0.0).astype(BF16)

    def main_pick(to_high):
        return picks((72, 128), lambda r, c: (r - 8 * odd) == (c - 64 * to_high),
                     lambda r, c: (c - 64 * to_high >= 0) & (c - 64 * to_high < 64))

    def tail_pick(to_high):
        return picks((16, 72), lambda r, c: c == (r - 8 * to_high) + 64 * (1 - odd),
                     lambda r, c: (r - 8 * to_high >= 0) & (r - 8 * to_high < 8))

    main_top, main_bottom = main_pick(odd), main_pick(1 - odd)
    tail_top, tail_bottom = tail_pick(odd), tail_pick(1 - odd)

    def chunk_rows(c, half):
        if c < 2:
            parts = [prompt[pl.ds(64 * (2 * q + half) + 32 * c, 32), :] for q in range(NX)]
        else:
            parts = [decode[2 * (c - 2) + s, pl.ds(16 * (2 * q + half), 16), :]
                     for q in range(NX) for s in range(2)]
        return jnp.concatenate(parts, axis=0)

    def pack(c):
        top, bottom = chunk_rows(c, 0), chunk_rows(c, 1)
        main = jnp.dot(top, main_top, preferred_element_type=F32)
        main += jnp.dot(bottom, main_bottom, preferred_element_type=F32)
        nt = (((1,), (1,)), ((), ()))
        tail = lax.dot_general(tail_top, top, nt, preferred_element_type=F32)
        tail += lax.dot_general(tail_bottom, bottom, nt, preferred_element_type=F32)
        pieces[c, z, y, 0:128, :] = main.astype(BF16)
        pieces[c, z, y, 128:144, :] = tail.astype(BF16)

    def ag(c, i):
        a_rows, b_rows = pl.ds(0, 64), pl.ds(64, 80)

        def piece(zi, yi, rows):
            return pieces.at[c, zi, yi, rows, :]

        if i in (0, 1):
            view = piece(z, y, a_rows)
        elif i == 2:
            view = piece(z, at_y(-1), pl.ds(0, 32))
        elif i == 3:
            view = piece(z, at_y(1), pl.ds(32, 32))
        elif i < 10:
            s = (i - 4) // 2
            view = piece(at_z(-s if i % 2 == 0 else s), slice(None), a_rows)
        elif i == 10:
            view = piece(at_z(-3), pl.ds(0, 2), a_rows)
        elif i == 11:
            view = piece(at_z(3), pl.ds(2, 2), a_rows)
        elif i < 18:
            s = (i - 12) // 2
            view = piece(at_z(-s if i % 2 == 0 else s), y, b_rows)
        elif i == 18:
            view = piece(at_z(-3), y, pl.ds(64, 48))
        elif i == 19:
            view = piece(at_z(3), y, pl.ds(112, 32))
        elif i in (20, 21):
            view = piece(slice(None), y, b_rows)
        elif i == 22:
            view = piece(pl.ds(0, 4), at_y(-1), b_rows)
        else:
            view = piece(pl.ds(4, 4), at_y(1), b_rows)
        on_y = i < 4 or i >= 20
        device = ((y_up, y_down) if on_y else (z_up, z_down))[i % 2]
        return pltpu.make_async_remote_copy(
            src_ref=view, dst_ref=view, send_sem=ag_send.at[c, i], recv_sem=ag_recv.at[c, i],
            device_id=device, device_id_type=MESH)

    stage_of = [(0, 1, 12, 13), (2, 3, 14, 15), (4, 5, 16, 17), (6, 7, 18, 19), (8, 9, 20, 21), (10, 11, 22, 23)]

    def gather_stage(c, k):
        if k == 0:
            pack(c)
            for i in stage_of[0]:
                ag(c, i).start()
            return
        if k == 6:
            for i in stage_of[5]:
                ag(c, i).wait_recv()
            return
        before, now = stage_of[k - 1], stage_of[k]
        for pair in (0, 2):
            crossing = (k == 2 and pair == 0) or (k == 4 and pair == 2)
            if crossing:
                ag(c, before[pair]).wait_recv()
                ag(c, before[pair + 1]).wait_recv()
                ag(c, now[pair]).start()
                ag(c, now[pair + 1]).start()
            else:
                for way in (0, 1):
                    ag(c, before[pair + way]).wait_recv()
                    ag(c, now[pair + way]).start()

    own_at = pl.multiple_of(core * 128, 128)
    other_at = pl.multiple_of((1 - core) * 128, 128)

    def unpack(c):
        low = lax.broadcasted_iota(jnp.int32, (128, 128), 1) < 64
        first = lax.broadcasted_iota(jnp.int32, (16, 128), 0) < 8

        def body(zi, carry):
            for yp in range(2):
                m = zi * 2 + yp
                e = pieces[c, zi, 2 * yp, 0:128, :].astype(F32)
                o = pieces[c, zi, 2 * yp + 1, 0:128, :].astype(F32)
                lanes = pl.ds(pl.multiple_of(m * 128, 128), 128)
                xs[pl.ds(own_at, 128), lanes] = jnp.where(low, e, o).astype(BF16)
                xs[pl.ds(other_at, 128), lanes] = pltpu.roll(jnp.where(low, o, e), 64, 1).astype(BF16)
                te = pieces[c, zi, 2 * yp, 128:144, :].astype(F32)
                to = pieces[c, zi, 2 * yp + 1, 128:144, :].astype(F32)
                tails[m, :, pl.ds(own_at, 128)] = jnp.where(first, te, to)
                tails[m, :, pl.ds(other_at, 128)] = pltpu.roll(jnp.where(first, to, te), 8, 0)
            return carry

        lax.fori_loop(0, NZ, body, 0)
        xs[:, 2048:2304] = tails[...].reshape(256, 256).T.astype(BF16)

    def rs(g, i):
        if i == 0:
            src, dst, device = psend.at[g], precv.at[g], other_core
        elif i < 3:
            src, dst, device = s1_out.at[g, i - 1], s1_in.at[g, i - 1], (x_down, x_up)[i - 1]
        else:
            src, dst, device = s2_out.at[g, i - 3], s2_in.at[g, i - 3], (x_down, x_up)[i - 3]
        return pltpu.make_async_remote_copy(
            src_ref=src, dst_ref=dst, send_sem=rs_send.at[g, i], recv_sem=rs_recv.at[g, i],
            device_id=device, device_id_type=MESH)

    def multiply(g):
        n = g % THIRDS

        def body(jj, carry):
            j = n * 3 + jj
            w_main = wbuf[j, :, 0:128, :].reshape(2048, 256)
            w_tail = wbuf[j, :, 128:144, :].reshape(256, 256)
            acc = jnp.dot(xs[:, 0:2048], w_main, preferred_element_type=F32)
            acc += jnp.dot(xs[:, 2048:2304], w_tail, preferred_element_type=F32)
            own[g % 4, jj] = acc[0:128]
            psend[g, jj] = acc[128:256].astype(BF16)
            return carry

        lax.fori_loop(0, 3, body, 0)
        rs(g, 0).start()

    def block(shift):
        return pl.ds(pl.multiple_of(at_x(shift) * 32, 32), 32)

    def reduce_1(g):
        rs(g, 0).wait_recv()
        total = own[g % 4] + precv[g].astype(F32)
        own[g % 4] = total
        far = own[g % 4, :, block(2), :].astype(BF16)
        s1_out[g, 0] = far[:, 0:16]
        s1_out[g, 1] = far[:, 16:32]
        rs(g, 1).start()
        rs(g, 2).start()

    def reduce_2(g):
        rs(g, 1).wait_recv()
        down = own[g % 4, :, block(-1), :]
        s2_out[g, 0, :, 0:16] = (down[:, 0:16] + s1_in[g, 0].astype(F32)).astype(BF16)
        s2_out[g, 0, :, 16:32] = down[:, 16:32].astype(BF16)
        rs(g, 3).start()
        rs(g, 2).wait_recv()
        above = own[g % 4, :, block(1), :]
        s2_out[g, 1, :, 0:16] = above[:, 0:16].astype(BF16)
        s2_out[g, 1, :, 16:32] = (above[:, 16:32] + s1_in[g, 1].astype(F32)).astype(BF16)
        rs(g, 4).start()

    def reduce_3(g):
        c, n = g // THIRDS, g % THIRDS
        rs(g, 3).wait_recv()
        rs(g, 4).wait_recv()
        total = own[g % 4, :, block(0), :] + s2_in[g, 0].astype(F32) + s2_in[g, 1].astype(F32)
        for jj in range(3):
            gate_sum, up_sum = total[jj, :, 0:128], total[jj, :, 128:256]
            hidden = (jax.nn.silu(gate_sum) * up_sum).astype(BF16)
            columns = pl.ds(128 * (3 * n + jj), 128)
            if c < 2:
                out_p[pl.ds(32 * c, 32), columns] = hidden
            else:
                out_d[2 * (c - 2), :, columns] = hidden[0:16]
                out_d[2 * (c - 2) + 1, :, columns] = hidden[16:32]

    def turn(g):
        c, n = g // THIRDS, g % THIRDS
        if g < GROUPS:
            if c == 0:
                for j in range(3 * n, 3 * n + 3):
                    pltpu.make_async_copy(wbuf.at[j], wbuf.at[j], w_sem.at[j]).wait()
            if n == 0:
                unpack(c)
            multiply(g)
        for back, step in ((1, reduce_1), (2, reduce_2), (3, reduce_3)):
            if 0 <= g - back < GROUPS:
                step(g - back)

    pl.semaphore_wait(barrier, 7)
    for t in range(13):
        events = [(c, t - 2 * c) for c in range(CHUNKS) if 0 <= t - 2 * c <= 6]
        ready = [3 * ((t - 7) // 2) + 1, 3 * ((t - 7) // 2) + 2] if t >= 7 and t % 2 else []
        for c, k in events:
            gather_stage(c, k)
            if ready:
                turn(ready.pop(0))
        for g in ready:
            turn(g)
        if t >= 6 and t % 2 == 0:
            turn(3 * ((t - 6) // 2))
    turn(10)
    turn(11)
    for g in range(GROUPS, GROUPS + 3):
        turn(g)

    for c in range(CHUNKS):
        for i in range(24):
            ag(c, i).wait_send()
    for g in range(GROUPS):
        for i in range(5):
            rs(g, i).wait_send()


def shards(prompt_tokens, decode_tokens, gate_weight, up_weight):
    gate_weight = gate_weight.reshape(16, 144, 1152)
    up_weight = up_weight.reshape(16, 144, 1152)
    vmem = pl.BlockSpec(memory_space=pltpu.VMEM)
    anywhere = pl.BlockSpec(memory_space=pl.ANY)
    return pl.pallas_call(
        kernel,
        out_shape=(jax.ShapeDtypeStruct((64, 1152), BF16), jax.ShapeDtypeStruct((4, 16, 1152), BF16)),
        in_specs=[vmem, vmem, anywhere, anywhere],
        out_specs=(vmem, vmem),
        scratch_shapes=[
            pltpu.VMEM((CHUNKS, NZ, NY, 144, 128), BF16),
            pltpu.VMEM((9, 16, 144, 256), BF16),
            pltpu.VMEM((256, 2304), BF16),
            pltpu.VMEM((16, 16, 256), F32),
            pltpu.VMEM((4, 3, 128, 256), F32),
            pltpu.VMEM((GROUPS, 3, 128, 256), BF16),
            pltpu.VMEM((GROUPS, 3, 128, 256), BF16),
            pltpu.VMEM((GROUPS, 2, 3, 16, 256), BF16),
            pltpu.VMEM((GROUPS, 2, 3, 16, 256), BF16),
            pltpu.VMEM((GROUPS, 2, 3, 32, 256), BF16),
            pltpu.VMEM((GROUPS, 2, 3, 32, 256), BF16),
            pltpu.SemaphoreType.DMA((CHUNKS, 24)),
            pltpu.SemaphoreType.DMA((CHUNKS, 24)),
            pltpu.SemaphoreType.DMA((GROUPS, 5)),
            pltpu.SemaphoreType.DMA((GROUPS, 5)),
            pltpu.SemaphoreType.DMA((9,)),
        ],
        compiler_params=pltpu.CompilerParams(
            collective_id=0, has_side_effects=True, vmem_limit_bytes=56 * 1024 * 1024),
        cost_estimate=pl.CostEstimate(flops=2 * 1024 * 2304 * 2304, bytes_accessed=11_000_000, transcendentals=147456),
    )(prompt_tokens, decode_tokens, gate_weight, up_weight)


def solution(mesh):
    in_specs = (P(None, ("gx", "gy")), P(None, None, ("gx", "gy")), P("gx", "gy"), P("gx", "gy"))
    out_specs = (P("gx", "gy"), P(None, "gx", "gy"))
    return jax.shard_map(shards, mesh=mesh, in_specs=in_specs, out_specs=out_specs, check_vma=False)
```

```python
import functools

import jax
import jax.numpy as jnp
from jax import lax
from jax.experimental import pallas as pl
from jax.experimental.pallas import tpu as pltpu
from jax.sharding import PartitionSpec as P

MESH = pl.DeviceIdType.MESH
NX, NZ, NY = 4, 8, 4
CHUNKS, THIRDS = 4, 3
GROUPS = CHUNKS * THIRDS
BF16, F32 = jnp.bfloat16, jnp.float32

SPLIT = (64, 32, 64, 64)
STRAIGHT = (False, False, False, False)
SETS = (((0, 3), (3, 5), (5, 8)), ((0, 3), (3, 8)), ((0, 3), (3, 5), (5, 8)), ((0, 8),))
SHORT = (11,)
ORDER = (
    ("pack", 0, 0), ("pack", 1, 0), ("B1", 0, 0), ("Y", 0, 0), ("B1", 1, 0), ("Y", 1, 0), ("A1", 0, 0), ("A1", 1, 0),
    ("pack", 2, 0), ("pack", 3, 0), ("B2", 0, 0), ("Y", 0, 1), ("B2", 1, 0), ("E", 0, 0), ("A2", 0, 0), ("E", 1, 0),
    ("A2", 1, 0), ("B1", 2, 0), ("Y", 2, 0), ("B1", 3, 0), ("A1", 2, 0), ("A1", 3, 0), ("Y", 0, 2), ("E", 0, 1),
    ("Y", 1, 1), ("A3", 0, 0), ("E", 2, 0), ("A3", 1, 0), ("B2", 2, 0), ("Y", 2, 1), ("B2", 3, 0), ("E", 0, 2),
    ("A2", 2, 0), ("A2", 3, 0), ("E", 1, 1), ("E", 2, 1), ("U", 0, 0), ("MM", 0, 0), ("MM", 1, 0), ("Y", 2, 2),
    ("Y", 3, 0), ("MM", 2, 0), ("R1", 0, 0), ("R1", 1, 0), ("A3", 2, 0), ("U", 1, 0), ("MM", 3, 0), ("R1", 2, 0),
    ("A3", 3, 0), ("MM", 4, 0), ("R2", 0, 0), ("R1", 3, 0), ("R2", 1, 0), ("E", 2, 2), ("MM", 5, 0), ("R1", 4, 0),
    ("R2", 2, 0), ("E", 3, 0), ("R1", 5, 0), ("R3", 0, 0), ("U", 2, 0), ("R2", 3, 0), ("MM", 6, 0), ("R3", 1, 0),
    ("R2", 4, 0), ("MM", 7, 0), ("R1", 6, 0), ("R3", 2, 0), ("R2", 5, 0), ("MM", 8, 0), ("R1", 7, 0), ("R3", 3, 0),
    ("U", 3, 0), ("MM", 9, 0), ("R1", 8, 0), ("R2", 6, 0), ("R3", 4, 0), ("MM", 10, 0), ("R2", 7, 0), ("R1", 9, 0),
    ("R3", 5, 0), ("MM", 11, 0), ("R1", 10, 0), ("R2", 8, 0), ("R3", 6, 0), ("R1", 11, 0), ("R3", 7, 0),
    ("R2", 9, 0), ("R2", 10, 0), ("R3", 8, 0), ("R3", 9, 0), ("R3", 10, 0), ("R3", 11, 0),
)

SLOT = {0: 0, -1: 1, 1: 2, -2: 3, 2: 4, -3: 5, 3: 6, 4: 7, -4: 7}
DISTANCE = (0, 1, 1, 2, 2, 3, 3, 4)


def rows_of(c, which):
    split = SPLIT[c]
    half = {96: 48, 80: 48, 112: 64, 128: 64}[144 - split]
    begin, size = {"a": (0, split), "b": (split, 144 - split), "low": (split, half), "high": (split + half, 144 - split - half)}[which]
    return pl.ds(begin, size)


def plan(c):
    copies = {"a1p": (0, 0, "a", 0, ("y", 1)), "a1m": (0, 0, "a", 0, ("y", -1)), "a1x": (0, 0, "a", 0, ("y", 2))}
    for s, way in ((1, "p"), (-1, "m")):
        for d in (1, 2, 3):
            copies[f"c{d}{way}"] = (SLOT[-s * (d - 1)], None, "a", SLOT[-s * d], ("z", s))
        copies[f"c4{way}"] = (SLOT[-2 * s], "pair" + way, "a", 7, ("z", 2 * s))
        if STRAIGHT[c]:
            for d in (1, 2, 3):
                copies[f"b{d}{way}"] = (0, 0, "b", SLOT[-s * d], ("z", s * d))
        else:
            for d in (1, 2, 3):
                copies[f"b{d}{way}"] = (SLOT[-s * (d - 1)], 0, "b", SLOT[-s * d], ("z", s))
            copies[f"b4{way}"] = (SLOT[-2 * s], 0, "low" if s > 0 else "high", 7, ("z", 2 * s))
        for i, (lo, hi) in enumerate(SETS[c]):
            copies[f"d{i}{way}"] = ((lo, hi), 0, "b", (lo, hi), ("y", s))
            copies[f"e{i}{way}"] = ((lo, hi), -s, "low" if s > 0 else "high", (lo, hi), ("y", s))
    if STRAIGHT[c]:
        copies["b4"] = (0, 0, "b", 7, ("z", 4))
    return copies


PLANS = [plan(c) for c in range(CHUNKS)]
COPY_INDEX = [{name: i for i, name in enumerate(p)} for p in PLANS]
MOST = max(len(p) for p in PLANS)


def steps(c):
    straight = STRAIGHT[c]
    table = {
        ("A1", 0): (("a1p", "a1m", "a1x"), ("c1p", "c1m")),
        ("A2", 0): (("c1p", "c1m"), ("c2p", "c2m")),
        ("A3", 0): (("c2p", "c2m"), ("c4p", "c4m", "c3p", "c3m")),
    }
    first = ["a1p", "a1m", "a1x"]
    if straight:
        first += ["b1p", "b1m", "b2p", "b2m", "b3p", "b3m", "b4"]
    else:
        first += ["b1p", "b1m"]
        table["B1", 0] = (("b1p", "b1m"), ("b2p", "b2m"))
        table["B2", 0] = (("b2p", "b2m"), ("b4p", "b4m", "b3p", "b3m"))
    table["pack", 0] = ((), tuple(first))
    done = ["c3p", "c3m", "c4p", "c4m"]
    for i, (lo, hi) in enumerate(SETS[c]):
        need = []
        for d in sorted(set(DISTANCE[lo:hi])):
            need += {0: [], 4: ["b4"] if straight else ["b4p", "b4m"]}.get(d, [f"b{d}p", f"b{d}m"])
        table["Y", i] = (tuple(need), (f"d{i}p", f"d{i}m"))
        table["E", i] = ((f"d{i}p", f"d{i}m"), (f"e{i}p", f"e{i}m"))
        done += [f"e{i}p", f"e{i}m"]
    table["U", 0] = (tuple(done), ())
    return table


STEPS = [steps(c) for c in range(CHUNKS)]


def kernel(prompt, decode, gate, up, out_p, out_d, pieces, wbuf, xs, tails, own, psend, precv,
           s1_out, s1_in, s2_out, s2_in, ag_send, ag_recv, rs_send, rs_recv, w_sem):
    gx, gy = lax.axis_index("gx"), lax.axis_index("gy")
    x, core = gx // 2, gx % 2
    z, y = gy // NY, gy % NY

    def at_y(shift):
        return lax.rem(y + (shift + NY), NY)

    def at_x(shift):
        return lax.rem(x + (shift + NX), NX)

    def device(axis, shift):
        if axis == "core":
            return {"gx": x * 2 + (1 - core), "gy": gy}
        if axis == "x":
            return {"gx": at_x(shift) * 2 + core, "gy": gy}
        if axis == "y":
            return {"gx": gx, "gy": z * NY + at_y(shift)}
        return {"gx": gx, "gy": lax.rem(z + (shift + NZ), NZ) * NY + y}

    barrier = pltpu.get_barrier_semaphore()
    hops = {("core", 1), ("x", 1), ("x", -1)} | {p[name][4] for p in PLANS for name in p}
    if SHORT:
        hops.add(("x", 2))
    for axis, shift in sorted(hops):
        pl.semaphore_signal(barrier, inc=1, device_id=device(axis, shift), device_id_type=MESH)

    for n in range(THIRDS):
        for half, source in enumerate((gate, up)):
            for begin, rows, to in ((0, 64, 0), (80, 64, 64), (64, 16, 128)):
                pltpu.make_async_copy(
                    source.at[:, pl.ds(begin, rows), pl.ds(384 * n, 384)],
                    wbuf.at[n, :, pl.ds(to, rows), pl.ds(384 * half, 384)],
                    w_sem.at[n],
                ).start()

    odd = y % 2
    nt = (((1,), (1,)), ((), ()))

    def picks(shape, row_of, col_of):
        r = lax.broadcasted_iota(jnp.int32, shape, 0)
        c = lax.broadcasted_iota(jnp.int32, shape, 1)
        return jnp.where(row_of(r, c) & col_of(r, c), 1.0, 0.0).astype(BF16)

    def main_pick(to_high):
        return picks((72, 128), lambda r, c: (r - 8 * odd) == (c - 64 * to_high),
                     lambda r, c: (c - 64 * to_high >= 0) & (c - 64 * to_high < 64))

    def tail_pick(to_high):
        return picks((16, 72), lambda r, c: c == (r - 8 * to_high) + 64 * (1 - odd),
                     lambda r, c: (r - 8 * to_high >= 0) & (r - 8 * to_high < 8))

    main_top, main_bottom = main_pick(odd), main_pick(1 - odd)
    tail_top, tail_bottom = tail_pick(odd), tail_pick(1 - odd)

    def chunk_rows(c, half):
        def row_pick(columns, source_of):
            r = lax.broadcasted_iota(jnp.int32, (128, columns), 0)
            s = lax.broadcasted_iota(jnp.int32, (128, columns), 1)
            return jnp.where(source_of(r) == s, 1.0, 0.0).astype(BF16)

        if c < 2:
            pick = row_pick(512, lambda r: (r // 32) * 128 + 64 * half + 32 * c + r % 32)
            got = lax.dot_general(pick, prompt[...], nt, preferred_element_type=F32)
        else:
            got = 0.0
            for s in range(2):
                pick = row_pick(128, lambda r: jnp.where((r % 32) // 16 == s, (r // 32) * 32 + 16 * half + r % 16, -1))
                got += lax.dot_general(pick, decode[2 * (c - 2) + s], nt, preferred_element_type=F32)
        return got.astype(BF16)

    def pack(c):
        top, bottom = chunk_rows(c, 0), chunk_rows(c, 1)
        main = jnp.dot(top, main_top, preferred_element_type=F32)
        main += jnp.dot(bottom, main_bottom, preferred_element_type=F32)
        tail = lax.dot_general(tail_top, top, nt, preferred_element_type=F32)
        tail += lax.dot_general(tail_bottom, bottom, nt, preferred_element_type=F32)
        pieces[c, 0, y, 0:128, :] = main.astype(BF16)
        pieces[c, 0, y, 128:144, :] = tail.astype(BF16)

    def copy(c, name):
        slots, y_shift, rows, to_slots, hop = PLANS[c][name]
        rows = rows_of(c, rows)
        if y_shift is None:
            y_at = slice(None)
        elif y_shift in ("pairp", "pairm"):
            y_at = pl.ds(0 if y_shift == "pairp" else 2, 2)
        else:
            y_at = at_y(y_shift)

        def view(s):
            s = pl.ds(s[0], s[1] - s[0]) if isinstance(s, tuple) else s
            return pieces.at[c, s, y_at, rows, :]

        i = COPY_INDEX[c][name]
        return pltpu.make_async_remote_copy(
            src_ref=view(slots), dst_ref=view(to_slots), send_sem=ag_send.at[c, i], recv_sem=ag_recv.at[c, i],
            device_id=device(*hop), device_id_type=MESH)

    top_at = pl.multiple_of(core * 128, 128)
    bottom_at = pl.multiple_of((1 - core) * 128, 128)

    def unpack(c):
        low = lax.broadcasted_iota(jnp.int32, (128, 128), 1) < 64
        first = lax.broadcasted_iota(jnp.int32, (16, 128), 0) < 8

        def body(slot, carry):
            away = (slot + 1) // 2
            source = lax.rem(z + jnp.where(slot % 2 == 0, away, NZ - away), NZ)
            for yp in range(2):
                m = source * 2 + yp
                e = pieces[c, slot, 2 * yp, 0:128, :].astype(F32)
                o = pieces[c, slot, 2 * yp + 1, 0:128, :].astype(F32)
                lanes = pl.ds(pl.multiple_of(m * 128, 128), 128)
                xs[pl.ds(top_at, 128), lanes] = jnp.where(low, e, o).astype(BF16)
                xs[pl.ds(bottom_at, 128), lanes] = pltpu.roll(jnp.where(low, o, e), 64, 1).astype(BF16)
                te = pieces[c, slot, 2 * yp, 128:144, :].astype(F32)
                to = pieces[c, slot, 2 * yp + 1, 128:144, :].astype(F32)
                tails[m, :, pl.ds(top_at, 128)] = jnp.where(first, te, to)
                tails[m, :, pl.ds(bottom_at, 128)] = pltpu.roll(jnp.where(first, to, te), 8, 0)
            return carry

        lax.fori_loop(0, NZ, body, 0)
        xs[:, 2048:2304] = tails[...].reshape(256, 256).T.astype(BF16)

    def rs(g, name):
        i = ("pair", "far_down", "far_up", "down", "up", "across").index(name)
        if i == 0:
            src, dst, to = psend.at[g], precv.at[g], ("core", 1)
        elif i < 3:
            src, dst, to = s1_out.at[g, i - 1], s1_in.at[g, i - 1], ("x", (-1, 1)[i - 1])
        else:
            src, dst, to = s2_out.at[g, i - 3], s2_in.at[g, i - 3], ("x", (-1, 1, 2)[i - 3])
        return pltpu.make_async_remote_copy(
            src_ref=src, dst_ref=dst, send_sem=rs_send.at[g, i], recv_sem=rs_recv.at[g, i],
            device_id=device(*to), device_id_type=MESH)

    def multiply(g):
        n = g % THIRDS
        if g < THIRDS:
            pltpu.make_async_copy(wbuf.at[n], wbuf.at[n], w_sem.at[n]).wait()
        acc = jnp.dot(xs[:, 0:2048], wbuf[n, :, 0:128, :].reshape(2048, 768), preferred_element_type=F32)
        acc += jnp.dot(xs[:, 2048:2304], wbuf[n, :, 128:144, :].reshape(256, 768), preferred_element_type=F32)
        psend[g] = acc[128:256].astype(BF16)
        rs(g, "pair").start()
        own[g % 6] = acc[0:128]

    def block(shift):
        return pl.ds(pl.multiple_of(at_x(shift) * 32, 32), 32)

    def reduce_1(g):
        rs(g, "pair").wait_recv()

        def pair_sum(shift):
            rows = block(shift)
            return own[g % 6, rows, :] + precv[g, rows, :].astype(F32)

        if g in SHORT:
            for i, (name, shift) in enumerate((("down", -1), ("up", 1), ("across", 2))):
                s2_out[g, i] = pair_sum(shift).astype(BF16)
            for name in ("across", "down", "up"):
                rs(g, name).start()
        else:
            far = pair_sum(2).astype(BF16)
            s1_out[g, 0] = far[0:16]
            s1_out[g, 1] = far[16:32]
            rs(g, "far_down").start()
            rs(g, "far_up").start()
            for shift in (-1, 1):
                own[g % 6, block(shift), :] = pair_sum(shift)
        own[g % 6, block(0), :] = pair_sum(0)

    def reduce_2(g):
        rs(g, "far_down").wait_recv()
        rs(g, "far_up").wait_recv()
        below, above = own[g % 6, block(-1), :], own[g % 6, block(1), :]
        s2_out[g, 0, 0:16] = (below[0:16] + s1_in[g, 0].astype(F32)).astype(BF16)
        s2_out[g, 0, 16:32] = below[16:32].astype(BF16)
        rs(g, "down").start()
        s2_out[g, 1, 0:16] = above[0:16].astype(BF16)
        s2_out[g, 1, 16:32] = (above[16:32] + s1_in[g, 1].astype(F32)).astype(BF16)
        rs(g, "up").start()

    def reduce_3(g):
        c, n = g // THIRDS, g % THIRDS
        rs(g, "down").wait_recv()
        rs(g, "up").wait_recv()
        total = own[g % 6, block(0), :] + s2_in[g, 0].astype(F32) + s2_in[g, 1].astype(F32)
        if g in SHORT:
            rs(g, "across").wait_recv()
            total += s2_in[g, 2].astype(F32)
        hidden = (jax.nn.silu(total[:, 0:384]) * total[:, 384:768]).astype(BF16)
        columns = pl.ds(384 * n, 384)
        if c < 2:
            out_p[pl.ds(32 * c, 32), columns] = hidden
        else:
            out_d[2 * (c - 2), :, columns] = hidden[0:16]
            out_d[2 * (c - 2) + 1, :, columns] = hidden[16:32]

    greeted, arrived = False, set()
    for kind, number, index in ORDER:
        if kind in ("MM", "R1", "R2", "R3"):
            {"MM": multiply, "R1": reduce_1, "R2": reduce_2, "R3": reduce_3}[kind](number)
            continue
        before, after = STEPS[number][kind, index]
        if kind == "pack":
            pack(number)
            if not greeted:
                pl.semaphore_wait(barrier, len(hops))
                greeted = True
        for name in before:
            if (number, name) not in arrived:
                copy(number, name).wait_recv()
                arrived.add((number, name))
        for name in after:
            copy(number, name).start()
        if kind == "U":
            unpack(number)

    for c in range(CHUNKS):
        for name in PLANS[c]:
            assert (c, name) in arrived
            copy(c, name).wait_send()
    for g in range(GROUPS):
        for name in ("pair", "down", "up") + (("across",) if g in SHORT else ("far_down", "far_up")):
            rs(g, name).wait_send()


def shards(prompt_tokens, decode_tokens, gate_weight, up_weight):
    gate_weight = gate_weight.reshape(16, 144, 1152)
    up_weight = up_weight.reshape(16, 144, 1152)
    vmem = pl.BlockSpec(memory_space=pltpu.VMEM)
    anywhere = pl.BlockSpec(memory_space=pl.ANY)
    return pl.pallas_call(
        kernel,
        out_shape=(jax.ShapeDtypeStruct((64, 1152), BF16), jax.ShapeDtypeStruct((4, 16, 1152), BF16)),
        in_specs=[vmem, vmem, anywhere, anywhere],
        out_specs=(vmem, vmem),
        scratch_shapes=[
            pltpu.VMEM((CHUNKS, NZ, NY, 144, 128), BF16),
            pltpu.VMEM((THIRDS, 16, 144, 768), BF16),
            pltpu.VMEM((256, 2304), BF16),
            pltpu.VMEM((16, 16, 256), F32),
            pltpu.VMEM((6, 128, 768), F32),
            pltpu.VMEM((GROUPS, 128, 768), BF16),
            pltpu.VMEM((GROUPS, 128, 768), BF16),
            pltpu.VMEM((GROUPS, 2, 16, 768), BF16),
            pltpu.VMEM((GROUPS, 2, 16, 768), BF16),
            pltpu.VMEM((GROUPS, 3, 32, 768), BF16),
            pltpu.VMEM((GROUPS, 3, 32, 768), BF16),
            pltpu.SemaphoreType.DMA((CHUNKS, MOST)),
            pltpu.SemaphoreType.DMA((CHUNKS, MOST)),
            pltpu.SemaphoreType.DMA((GROUPS, 6)),
            pltpu.SemaphoreType.DMA((GROUPS, 6)),
            pltpu.SemaphoreType.DMA((THIRDS,)),
        ],
        compiler_params=pltpu.CompilerParams(
            collective_id=0, has_side_effects=True, vmem_limit_bytes=56 * 1024 * 1024),
        cost_estimate=pl.CostEstimate(flops=2 * 1024 * 2304 * 2304, bytes_accessed=11_000_000, transcendentals=147456),
    )(prompt_tokens.T, decode_tokens.transpose(0, 2, 1), gate_weight, up_weight)


def solution(mesh):
    in_specs = (P(None, ("gx", "gy")), P(None, None, ("gx", "gy")), P("gx", "gy"), P("gx", "gy"))
    out_specs = (P("gx", "gy"), P(None, "gx", "gy"))
    return jax.shard_map(shards, mesh=mesh, in_specs=in_specs, out_specs=out_specs, check_vma=False)
```

```python
import functools

import jax
import jax.numpy as jnp
from jax import lax
from jax.experimental import pallas as pl
from jax.experimental.pallas import tpu as pltpu
from jax.sharding import PartitionSpec as P

MESH = pl.DeviceIdType.MESH
NX, NZ, NY = 4, 8, 4
CHUNKS, THIRDS = 4, 3
GROUPS = CHUNKS * THIRDS
BF16, F32 = jnp.bfloat16, jnp.float32

SPLIT = (32, 64, 48, 48)
STRAIGHT = (True, True, False, False)
SETS = (((0, 5), (5, 8)), ((0, 5), (5, 8)), ((0, 5), (5, 8)), ((0, 3), (3, 5), (5, 8)))
WIDE = (False, False, False, False)
LEAP = (False, False, False, False)
SHORT = (8, 9, 10, 11)
ORDER = (
    ("pack", 0, 0), ("A1", 0, 0), ("pack", 1, 0), ("pack", 2, 0), ("Y", 0, 0), ("A2", 0, 0), ("Y", 0, 1),
    ("A1", 1, 0), ("Y", 1, 0), ("A1", 2, 0), ("pack", 3, 0), ("E", 0, 0), ("B1", 2, 0), ("A3", 0, 0), ("E", 0, 1),
    ("A2", 1, 0), ("Y", 1, 1), ("A2", 2, 0), ("B2", 2, 0), ("E", 1, 0), ("A1", 3, 0), ("Y", 2, 0), ("B1", 3, 0),
    ("U", 0, 0), ("A3", 1, 0), ("MM", 0, 0), ("E", 1, 1), ("MM", 1, 0), ("Y", 2, 1), ("A3", 2, 0), ("R1", 0, 0),
    ("MM", 2, 0), ("R1", 1, 0), ("E", 2, 0), ("A2", 3, 0), ("B2", 3, 0), ("Y", 3, 0), ("R1", 2, 0), ("U", 1, 0),
    ("R2", 0, 0), ("Y", 3, 1), ("MM", 3, 0), ("R2", 1, 0), ("E", 2, 1), ("MM", 4, 0), ("R2", 2, 0), ("R1", 3, 0),
    ("A3", 3, 0), ("Y", 3, 2), ("MM", 5, 0), ("R1", 4, 0), ("E", 3, 0), ("R3", 0, 0), ("U", 2, 0), ("E", 3, 1),
    ("R1", 5, 0), ("R3", 1, 0), ("MM", 6, 0), ("R2", 3, 0), ("R3", 2, 0), ("E", 3, 2), ("MM", 7, 0), ("R2", 4, 0),
    ("R1", 6, 0), ("MM", 8, 0), ("R2", 5, 0), ("R1", 7, 0), ("U", 3, 0), ("R1", 8, 0), ("R3", 3, 0), ("MM", 9, 0),
    ("R2", 6, 0), ("R3", 4, 0), ("MM", 10, 0), ("R2", 7, 0), ("R1", 9, 0), ("R3", 5, 0), ("MM", 11, 0),
    ("R1", 10, 0), ("R3", 6, 0), ("R1", 11, 0), ("R3", 7, 0), ("R3", 8, 0), ("R3", 9, 0), ("R3", 10, 0),
    ("R3", 11, 0),
)

SLOT = {0: 0, -1: 1, 1: 2, -2: 3, 2: 4, -3: 5, 3: 6, 4: 7, -4: 7}
DISTANCE = (0, 1, 1, 2, 2, 3, 3, 4)


def rows_of(c, which):
    split = SPLIT[c]
    half = {96: 48, 80: 48, 112: 64, 128: 64}[144 - split]
    begin, size = {"a": (0, split), "b": (split, 144 - split), "low": (split, half), "high": (split + half, 144 - split - half)}[which]
    return pl.ds(begin, size)


def plan(c):
    copies = {"a1p": (0, 0, "a", 0, ("y", 1)), "a1m": (0, 0, "a", 0, ("y", -1)), "a1x": (0, 0, "a", 0, ("y", 2))}
    for s, way in ((1, "p"), (-1, "m")):
        for d in (1, 2, 3):
            leap = 2 if d == 2 and LEAP[c] else 1
            copies[f"c{d}{way}"] = (SLOT[-s * (d - leap)], None, "a", SLOT[-s * d], ("z", s * leap))
        copies[f"c4{way}"] = (SLOT[-2 * s], "pair" + way, "a", 7, ("z", 2 * s))
        if STRAIGHT[c]:
            for d in (1, 2, 3):
                copies[f"b{d}{way}"] = (0, 0, "b", SLOT[-s * d], ("z", s * d))
        else:
            for d in (1, 2, 3):
                copies[f"b{d}{way}"] = (SLOT[-s * (d - 1)], 0, "b", SLOT[-s * d], ("z", s))
            copies[f"b4{way}"] = (SLOT[-2 * s], 0, "low" if s > 0 else "high", 7, ("z", 2 * s))
        for i, (lo, hi) in enumerate(SETS[c]):
            copies[f"d{i}{way}"] = ((lo, hi), 0, "b", (lo, hi), ("y", s))
            if WIDE[c]:
                copies[f"x{i}"] = ((lo, hi), 0, "b", (lo, hi), ("y", 2))
            else:
                copies[f"e{i}{way}"] = ((lo, hi), -s, "low" if s > 0 else "high", (lo, hi), ("y", s))
    if STRAIGHT[c]:
        copies["b4"] = (0, 0, "b", 7, ("z", 4))
    return copies


PLANS = [plan(c) for c in range(CHUNKS)]
COPY_INDEX = [{name: i for i, name in enumerate(p)} for p in PLANS]
MOST = max(len(p) for p in PLANS)


def steps(c):
    straight = STRAIGHT[c]
    table = {
        ("A1", 0): (("a1p", "a1m", "a1x"), ("c1p", "c1m")),
        ("A2", 0): (("c1p", "c1m"), ("c2p", "c2m")),
        ("A3", 0): (("c2p", "c2m"), ("c4p", "c4m", "c3p", "c3m")),
    }
    if LEAP[c]:
        table["A1", 0] = (("a1p", "a1m", "a1x"), ("c2p", "c2m", "c1p", "c1m"))
        del table["A2", 0]
    first = ["a1p", "a1m", "a1x"]
    if straight:
        first += ["b1p", "b1m", "b2p", "b2m", "b3p", "b3m", "b4"]
    else:
        first += ["b1p", "b1m"]
        table["B1", 0] = (("b1p", "b1m"), ("b2p", "b2m"))
        table["B2", 0] = (("b2p", "b2m"), ("b4p", "b4m", "b3p", "b3m"))
    table["pack", 0] = ((), tuple(first))
    done = ["c1p", "c1m", "c3p", "c3m", "c4p", "c4m"]
    for i, (lo, hi) in enumerate(SETS[c]):
        need = []
        for d in sorted(set(DISTANCE[lo:hi])):
            need += {0: [], 4: ["b4"] if straight else ["b4p", "b4m"]}.get(d, [f"b{d}p", f"b{d}m"])
        if WIDE[c]:
            table["Y", i] = (tuple(need), (f"x{i}", f"d{i}p", f"d{i}m"))
            done += [f"d{i}p", f"d{i}m", f"x{i}"]
        else:
            table["Y", i] = (tuple(need), (f"d{i}p", f"d{i}m"))
            table["E", i] = ((f"d{i}p", f"d{i}m"), (f"e{i}p", f"e{i}m"))
            done += [f"e{i}p", f"e{i}m"]
    table["U", 0] = (tuple(done), ())
    return table


STEPS = [steps(c) for c in range(CHUNKS)]


def kernel(prompt, decode, gate, up, out_p, out_d, pieces, wbuf, xs, tails, own, psend, precv,
           s1_out, s1_in, s2_out, s2_in, ag_send, ag_recv, rs_send, rs_recv, w_sem):
    gx, gy = lax.axis_index("gx"), lax.axis_index("gy")
    x, core = gx // 2, gx % 2
    z, y = gy // NY, gy % NY

    def at_y(shift):
        return lax.rem(y + (shift + NY), NY)

    def at_x(shift):
        return lax.rem(x + (shift + NX), NX)

    def device(axis, shift):
        if axis == "core":
            return {"gx": x * 2 + (1 - core), "gy": gy}
        if axis == "x":
            return {"gx": at_x(shift) * 2 + core, "gy": gy}
        if axis == "y":
            return {"gx": gx, "gy": z * NY + at_y(shift)}
        return {"gx": gx, "gy": lax.rem(z + (shift + NZ), NZ) * NY + y}

    barrier = pltpu.get_barrier_semaphore()
    hops = {("core", 1), ("x", 1), ("x", -1)} | {p[name][4] for p in PLANS for name in p}
    if SHORT:
        hops.add(("x", 2))
    for axis, shift in sorted(hops):
        pl.semaphore_signal(barrier, inc=1, device_id=device(axis, shift), device_id_type=MESH)

    for n in range(THIRDS):
        for half, source in enumerate((gate, up)):
            for begin, rows, to in ((0, 64, 0), (80, 64, 64), (64, 16, 128)):
                pltpu.make_async_copy(
                    source.at[:, pl.ds(begin, rows), pl.ds(384 * n, 384)],
                    wbuf.at[n, :, pl.ds(to, rows), pl.ds(384 * half, 384)],
                    w_sem.at[n],
                ).start()

    odd = y % 2
    nt = (((1,), (1,)), ((), ()))

    def picks(shape, row_of, col_of):
        r = lax.broadcasted_iota(jnp.int32, shape, 0)
        c = lax.broadcasted_iota(jnp.int32, shape, 1)
        return jnp.where(row_of(r, c) & col_of(r, c), 1.0, 0.0).astype(BF16)

    def main_pick(to_high):
        return picks((72, 128), lambda r, c: (r - 8 * odd) == (c - 64 * to_high),
                     lambda r, c: (c - 64 * to_high >= 0) & (c - 64 * to_high < 64))

    def tail_pick(to_high):
        return picks((16, 72), lambda r, c: c == (r - 8 * to_high) + 64 * (1 - odd),
                     lambda r, c: (r - 8 * to_high >= 0) & (r - 8 * to_high < 8))

    main_top, main_bottom = main_pick(odd), main_pick(1 - odd)
    tail_top, tail_bottom = tail_pick(odd), tail_pick(1 - odd)

    def chunk_rows(c, half):
        def row_pick(columns, source_of):
            r = lax.broadcasted_iota(jnp.int32, (128, columns), 0)
            s = lax.broadcasted_iota(jnp.int32, (128, columns), 1)
            return jnp.where(source_of(r) == s, 1.0, 0.0).astype(BF16)

        if c < 2:
            pick = row_pick(512, lambda r: (r // 32) * 128 + 64 * half + 32 * c + r % 32)
            got = lax.dot_general(pick, prompt[...], nt, preferred_element_type=F32)
        else:
            got = 0.0
            for s in range(2):
                pick = row_pick(128, lambda r: jnp.where((r % 32) // 16 == s, (r // 32) * 32 + 16 * half + r % 16, -1))
                got += lax.dot_general(pick, decode[2 * (c - 2) + s], nt, preferred_element_type=F32)
        return got.astype(BF16)

    def pack(c):
        top, bottom = chunk_rows(c, 0), chunk_rows(c, 1)
        main = jnp.dot(top, main_top, preferred_element_type=F32)
        main += jnp.dot(bottom, main_bottom, preferred_element_type=F32)
        tail = lax.dot_general(tail_top, top, nt, preferred_element_type=F32)
        tail += lax.dot_general(tail_bottom, bottom, nt, preferred_element_type=F32)
        pieces[c, 0, y, 0:128, :] = main.astype(BF16)
        pieces[c, 0, y, 128:144, :] = tail.astype(BF16)

    def copy(c, name):
        slots, y_shift, rows, to_slots, hop = PLANS[c][name]
        rows = rows_of(c, rows)
        if y_shift is None:
            y_at = slice(None)
        elif y_shift in ("pairp", "pairm"):
            y_at = pl.ds(0 if y_shift == "pairp" else 2, 2)
        else:
            y_at = at_y(y_shift)

        def view(s):
            s = pl.ds(s[0], s[1] - s[0]) if isinstance(s, tuple) else s
            return pieces.at[c, s, y_at, rows, :]

        i = COPY_INDEX[c][name]
        return pltpu.make_async_remote_copy(
            src_ref=view(slots), dst_ref=view(to_slots), send_sem=ag_send.at[c, i], recv_sem=ag_recv.at[c, i],
            device_id=device(*hop), device_id_type=MESH)

    top_at = pl.multiple_of(core * 128, 128)
    bottom_at = pl.multiple_of((1 - core) * 128, 128)

    def unpack(c):
        low = lax.broadcasted_iota(jnp.int32, (128, 128), 1) < 64
        first = lax.broadcasted_iota(jnp.int32, (16, 128), 0) < 8
        def body(slot, carry):
            away = (slot + 1) // 2
            source = lax.rem(z + jnp.where(slot % 2 == 0, away, NZ - away), NZ)
            for yp in range(2):
                m = source * 2 + yp
                e = pieces[c, slot, 2 * yp, 0:128, :]
                o = pieces[c, slot, 2 * yp + 1, 0:128, :]
                lanes = pl.ds(pl.multiple_of(m * 128, 128), 128)
                xs[pl.ds(top_at, 128), lanes] = jnp.where(low, e, o)
                xs[pl.ds(bottom_at, 128), lanes] = pltpu.roll(jnp.where(low, o, e), 64, 1)
                te = pieces[c, slot, 2 * yp, 128:144, :].astype(F32)
                to = pieces[c, slot, 2 * yp + 1, 128:144, :].astype(F32)
                tails[m, :, pl.ds(top_at, 128)] = jnp.where(first, te, to)
                tails[m, :, pl.ds(bottom_at, 128)] = pltpu.roll(jnp.where(first, to, te), 8, 0)
            return carry

        lax.fori_loop(0, NZ, body, 0)
        xs[:, 2048:2304] = tails[...].reshape(256, 256).T.astype(BF16)

    def rs(g, name):
        i = ("pair", "far_down", "far_up", "down", "up", "across").index(name)
        if i == 0:
            src, dst, to = psend.at[g], precv.at[g], ("core", 1)
        elif i < 3:
            src, dst, to = s1_out.at[g, i - 1], s1_in.at[g, i - 1], ("x", (-1, 1)[i - 1])
        else:
            src, dst, to = s2_out.at[g, i - 3], s2_in.at[g, i - 3], ("x", (-1, 1, 2)[i - 3])
        return pltpu.make_async_remote_copy(
            src_ref=src, dst_ref=dst, send_sem=rs_send.at[g, i], recv_sem=rs_recv.at[g, i],
            device_id=device(*to), device_id_type=MESH)

    def multiply(g):
        n = lax.rem(g, THIRDS)

        @pl.when(g < THIRDS)
        def _():
            pltpu.make_async_copy(wbuf.at[n], wbuf.at[n], w_sem.at[n]).wait()

        @pl.when(n == 0)
        def _():
            unpack(g // THIRDS)

        acc = jnp.dot(xs[:, 0:2048], wbuf[n, :, 0:128, :].reshape(2048, 768), preferred_element_type=F32)
        acc += jnp.dot(xs[:, 2048:2304], wbuf[n, :, 128:144, :].reshape(256, 768), preferred_element_type=F32)
        psend[g] = acc[128:256].astype(BF16)
        rs(g, "pair").start()
        own[lax.rem(g, 6)] = acc[0:128]

    def block(shift):
        return pl.ds(pl.multiple_of(at_x(shift) * 32, 32), 32)

    def reduce_1(g):
        rs(g, "pair").wait_recv()

        def pair_sum(shift):
            rows = block(shift)
            return own[g % 6, rows, :] + precv[g, rows, :].astype(F32)

        if g in SHORT:
            for i, (name, shift) in enumerate((("down", -1), ("up", 1), ("across", 2))):
                s2_out[g, i] = pair_sum(shift).astype(BF16)
            for name in ("across", "down", "up"):
                rs(g, name).start()
        else:
            far = pair_sum(2).astype(BF16)
            s1_out[g, 0] = far[0:16]
            s1_out[g, 1] = far[16:32]
            rs(g, "far_down").start()
            rs(g, "far_up").start()
            for shift in (-1, 1):
                own[g % 6, block(shift), :] = pair_sum(shift)
        own[g % 6, block(0), :] = pair_sum(0)

    def reduce_2(g):
        rs(g, "far_down").wait_recv()
        rs(g, "far_up").wait_recv()
        below, above = own[g % 6, block(-1), :], own[g % 6, block(1), :]
        s2_out[g, 0, 0:16] = (below[0:16] + s1_in[g, 0].astype(F32)).astype(BF16)
        s2_out[g, 0, 16:32] = below[16:32].astype(BF16)
        rs(g, "down").start()
        s2_out[g, 1, 0:16] = above[0:16].astype(BF16)
        s2_out[g, 1, 16:32] = (above[16:32] + s1_in[g, 1].astype(F32)).astype(BF16)
        rs(g, "up").start()

    def reduce_3(g):
        c, n = g // THIRDS, g % THIRDS
        rs(g, "down").wait_recv()
        rs(g, "up").wait_recv()
        total = own[g % 6, block(0), :] + s2_in[g, 0].astype(F32) + s2_in[g, 1].astype(F32)
        if g in SHORT:
            rs(g, "across").wait_recv()
            total += s2_in[g, 2].astype(F32)
        hidden = (jax.nn.silu(total[:, 0:384]) * total[:, 384:768]).astype(BF16)
        columns = pl.ds(384 * n, 384)
        if c < 2:
            out_p[pl.ds(32 * c, 32), columns] = hidden
        else:
            out_d[2 * (c - 2), :, columns] = hidden[0:16]
            out_d[2 * (c - 2) + 1, :, columns] = hidden[16:32]

    arrived = set()

    def perform(kind, number, index):
        if kind in ("R1", "R2", "R3"):
            {"R1": reduce_1, "R2": reduce_2, "R3": reduce_3}[kind](number)
            return
        before, after = STEPS[number][kind, index]
        if kind == "pack":
            pack(number)
        for name in before:
            if (number, name) not in arrived:
                copy(number, name).wait_recv()
                arrived.add((number, name))
        for name in after:
            copy(number, name).start()

    between = [[]]
    for kind, number, index in ORDER:
        if kind == "MM":
            between.append([])
        else:
            between[-1].append((kind, number, index))
    pack(0)
    pl.semaphore_wait(barrier, len(hops))
    for name in STEPS[0]["pack", 0][1]:
        copy(0, name).start()
    between[0].remove(("pack", 0, 0))
    for work in between[0]:
        perform(*work)

    def round_of(g, carry):
        multiply(g)

        def follow(lo, hi):
            if hi - lo == 1:
                for work in between[lo + 1]:
                    perform(*work)
                return
            middle = (lo + hi) // 2

            @pl.when(g < middle)
            def _():
                follow(lo, middle)

            @pl.when(g >= middle)
            def _():
                follow(middle, hi)

        follow(0, GROUPS)
        return carry

    lax.fori_loop(0, GROUPS, round_of, 0)
    for c in range(CHUNKS):
        for name in PLANS[c]:
            assert (c, name) in arrived
            copy(c, name).wait_send()
    for g in range(GROUPS):
        for name in ("pair", "down", "up") + (("across",) if g in SHORT else ("far_down", "far_up")):
            rs(g, name).wait_send()


def shards(prompt_tokens, decode_tokens, gate_weight, up_weight):
    gate_weight = gate_weight.reshape(16, 144, 1152)
    up_weight = up_weight.reshape(16, 144, 1152)
    vmem = pl.BlockSpec(memory_space=pltpu.VMEM)
    anywhere = pl.BlockSpec(memory_space=pl.ANY)
    return pl.pallas_call(
        kernel,
        out_shape=(jax.ShapeDtypeStruct((64, 1152), BF16), jax.ShapeDtypeStruct((4, 16, 1152), BF16)),
        in_specs=[vmem, vmem, anywhere, anywhere],
        out_specs=(vmem, vmem),
        scratch_shapes=[
            pltpu.VMEM((CHUNKS, NZ, NY, 144, 128), BF16),
            pltpu.VMEM((THIRDS, 16, 144, 768), BF16),
            pltpu.VMEM((256, 2304), BF16),
            pltpu.VMEM((16, 16, 256), F32),
            pltpu.VMEM((6, 128, 768), F32),
            pltpu.VMEM((GROUPS, 128, 768), BF16),
            pltpu.VMEM((GROUPS, 128, 768), BF16),
            pltpu.VMEM((GROUPS, 2, 16, 768), BF16),
            pltpu.VMEM((GROUPS, 2, 16, 768), BF16),
            pltpu.VMEM((GROUPS, 3, 32, 768), BF16),
            pltpu.VMEM((GROUPS, 3, 32, 768), BF16),
            pltpu.SemaphoreType.DMA((CHUNKS, MOST)),
            pltpu.SemaphoreType.DMA((CHUNKS, MOST)),
            pltpu.SemaphoreType.DMA((GROUPS, 6)),
            pltpu.SemaphoreType.DMA((GROUPS, 6)),
            pltpu.SemaphoreType.DMA((THIRDS,)),
        ],
        compiler_params=pltpu.CompilerParams(
            collective_id=0, has_side_effects=True, vmem_limit_bytes=56 * 1024 * 1024),
        cost_estimate=pl.CostEstimate(flops=2 * 1024 * 2304 * 2304, bytes_accessed=11_000_000, transcendentals=147456),
    )(prompt_tokens.T, decode_tokens.transpose(0, 2, 1), gate_weight, up_weight)


def solution(mesh):
    in_specs = (P(None, ("gx", "gy")), P(None, None, ("gx", "gy")), P("gx", "gy"), P("gx", "gy"))
    out_specs = (P("gx", "gy"), P(None, "gx", "gy"))
    return jax.shard_map(shards, mesh=mesh, in_specs=in_specs, out_specs=out_specs, check_vma=False)
```

```python
import functools

import jax
import jax.numpy as jnp
from jax import lax
from jax.experimental import pallas as pl
from jax.experimental.pallas import tpu as pltpu
from jax.sharding import PartitionSpec as P

MESH = pl.DeviceIdType.MESH
NX, NZ, NY = 4, 8, 4
CHUNKS, THIRDS = 4, 3
GROUPS = CHUNKS * THIRDS
BF16, F32 = jnp.bfloat16, jnp.float32

SPLIT = (32, 64, 48, 48)
STRAIGHT = (True, True, False, False)
SETS = (((0, 5), (5, 8)), ((0, 5), (5, 8)), ((0, 5), (5, 8)), ((0, 3), (3, 5), (5, 8)))
WIDE = (False, False, False, False)
LEAP = (False, False, False, False)
SHORT = (8, 9, 10, 11)
ORDER = (
    ("pack", 0, 0), ("A1", 0, 0), ("pack", 1, 0), ("pack", 2, 0), ("Y", 0, 0), ("A2", 0, 0), ("Y", 0, 1),
    ("A1", 1, 0), ("Y", 1, 0), ("A1", 2, 0), ("pack", 3, 0), ("E", 0, 0), ("B1", 2, 0), ("A3", 0, 0), ("E", 0, 1),
    ("A2", 1, 0), ("Y", 1, 1), ("A2", 2, 0), ("B2", 2, 0), ("E", 1, 0), ("A1", 3, 0), ("Y", 2, 0), ("B1", 3, 0),
    ("U", 0, 0), ("A3", 1, 0), ("MM", 0, 0), ("E", 1, 1), ("MM", 1, 0), ("Y", 2, 1), ("A3", 2, 0), ("R1", 0, 0),
    ("MM", 2, 0), ("R1", 1, 0), ("E", 2, 0), ("A2", 3, 0), ("B2", 3, 0), ("Y", 3, 0), ("R1", 2, 0), ("U", 1, 0),
    ("R2", 0, 0), ("Y", 3, 1), ("MM", 3, 0), ("R2", 1, 0), ("E", 2, 1), ("MM", 4, 0), ("R2", 2, 0), ("R1", 3, 0),
    ("A3", 3, 0), ("Y", 3, 2), ("MM", 5, 0), ("R1", 4, 0), ("E", 3, 0), ("R3", 0, 0), ("U", 2, 0), ("E", 3, 1),
    ("R1", 5, 0), ("R3", 1, 0), ("MM", 6, 0), ("R2", 3, 0), ("R3", 2, 0), ("E", 3, 2), ("MM", 7, 0), ("R2", 4, 0),
    ("R1", 6, 0), ("MM", 8, 0), ("R2", 5, 0), ("R1", 7, 0), ("U", 3, 0), ("R1", 8, 0), ("R3", 3, 0), ("MM", 9, 0),
    ("R2", 6, 0), ("R3", 4, 0), ("MM", 10, 0), ("R2", 7, 0), ("R1", 9, 0), ("R3", 5, 0), ("MM", 11, 0),
    ("R1", 10, 0), ("R3", 6, 0), ("R1", 11, 0), ("R3", 7, 0), ("R3", 8, 0), ("R3", 9, 0), ("R3", 10, 0),
    ("R3", 11, 0),
)

SLOT = {0: 0, -1: 1, 1: 2, -2: 3, 2: 4, -3: 5, 3: 6, 4: 7, -4: 7}
DISTANCE = (0, 1, 1, 2, 2, 3, 3, 4)


def rows_of(c, which):
    split = SPLIT[c]
    half = {96: 48, 80: 48, 112: 64, 128: 64}[144 - split]
    begin, size = {"a": (0, split), "b": (split, 144 - split), "low": (split, half), "high": (split + half, 144 - split - half)}[which]
    return pl.ds(begin, size)


def plan(c):
    copies = {"a1p": (0, 0, "a", 0, ("y", 1)), "a1m": (0, 0, "a", 0, ("y", -1)), "a1x": (0, 0, "a", 0, ("y", 2))}
    for s, way in ((1, "p"), (-1, "m")):
        for d in (1, 2, 3):
            leap = 2 if d == 2 and LEAP[c] else 1
            copies[f"c{d}{way}"] = (SLOT[-s * (d - leap)], None, "a", SLOT[-s * d], ("z", s * leap))
        copies[f"c4{way}"] = (SLOT[-2 * s], "pair" + way, "a", 7, ("z", 2 * s))
        if STRAIGHT[c]:
            for d in (1, 2, 3):
                copies[f"b{d}{way}"] = (0, 0, "b", SLOT[-s * d], ("z", s * d))
        else:
            for d in (1, 2, 3):
                copies[f"b{d}{way}"] = (SLOT[-s * (d - 1)], 0, "b", SLOT[-s * d], ("z", s))
            copies[f"b4{way}"] = (SLOT[-2 * s], 0, "low" if s > 0 else "high", 7, ("z", 2 * s))
        for i, (lo, hi) in enumerate(SETS[c]):
            copies[f"d{i}{way}"] = ((lo, hi), 0, "b", (lo, hi), ("y", s))
            if WIDE[c]:
                copies[f"x{i}"] = ((lo, hi), 0, "b", (lo, hi), ("y", 2))
            else:
                copies[f"e{i}{way}"] = ((lo, hi), -s, "low" if s > 0 else "high", (lo, hi), ("y", s))
    if STRAIGHT[c]:
        copies["b4"] = (0, 0, "b", 7, ("z", 4))
    return copies


PLANS = [plan(c) for c in range(CHUNKS)]
COPY_INDEX = [{name: i for i, name in enumerate(p)} for p in PLANS]
MOST = max(len(p) for p in PLANS)


def steps(c):
    straight = STRAIGHT[c]
    table = {
        ("A1", 0): (("a1p", "a1m", "a1x"), ("c1p", "c1m")),
        ("A2", 0): (("c1p", "c1m"), ("c2p", "c2m")),
        ("A3", 0): (("c2p", "c2m"), ("c4p", "c4m", "c3p", "c3m")),
    }
    if LEAP[c]:
        table["A1", 0] = (("a1p", "a1m", "a1x"), ("c2p", "c2m", "c1p", "c1m"))
        del table["A2", 0]
    first = ["a1p", "a1m", "a1x"]
    if straight:
        first += ["b1p", "b1m", "b2p", "b2m", "b3p", "b3m", "b4"]
    else:
        first += ["b1p", "b1m"]
        table["B1", 0] = (("b1p", "b1m"), ("b2p", "b2m"))
        table["B2", 0] = (("b2p", "b2m"), ("b4p", "b4m", "b3p", "b3m"))
    table["pack", 0] = ((), tuple(first))
    done = ["c1p", "c1m", "c3p", "c3m", "c4p", "c4m"]
    for i, (lo, hi) in enumerate(SETS[c]):
        need = []
        for d in sorted(set(DISTANCE[lo:hi])):
            need += {0: [], 4: ["b4"] if straight else ["b4p", "b4m"]}.get(d, [f"b{d}p", f"b{d}m"])
        if WIDE[c]:
            table["Y", i] = (tuple(need), (f"x{i}", f"d{i}p", f"d{i}m"))
            done += [f"d{i}p", f"d{i}m", f"x{i}"]
        else:
            table["Y", i] = (tuple(need), (f"d{i}p", f"d{i}m"))
            table["E", i] = ((f"d{i}p", f"d{i}m"), (f"e{i}p", f"e{i}m"))
            done += [f"e{i}p", f"e{i}m"]
    table["U", 0] = (tuple(done), ())
    return table


STEPS = [steps(c) for c in range(CHUNKS)]


def kernel(prompt, decode, gate, up, out, pieces, wbuf, xs, tails, own, psend, precv,
           s1_out, s1_in, s2_out, s2_in, ag_send, ag_recv, rs_send, rs_recv, w_sem):
    gx, gy = lax.axis_index("gx"), lax.axis_index("gy")
    x, core = gx // 2, gx % 2
    z, y = gy // NY, gy % NY

    def at_y(shift):
        return lax.rem(y + (shift + NY), NY)

    def at_x(shift):
        return lax.rem(x + (shift + NX), NX)

    def device(axis, shift):
        if axis == "core":
            return {"gx": x * 2 + (1 - core), "gy": gy}
        if axis == "x":
            return {"gx": at_x(shift) * 2 + core, "gy": gy}
        if axis == "y":
            return {"gx": gx, "gy": z * NY + at_y(shift)}
        return {"gx": gx, "gy": lax.rem(z + (shift + NZ), NZ) * NY + y}

    barrier = pltpu.get_barrier_semaphore()
    hops = {("core", 1), ("x", 1), ("x", -1)} | {p[name][4] for p in PLANS for name in p}
    if SHORT:
        hops.add(("x", 2))
    for axis, shift in sorted(hops):
        pl.semaphore_signal(barrier, inc=1, device_id=device(axis, shift), device_id_type=MESH)

    for n in range(THIRDS):
        for half, source in enumerate((gate, up)):
            for begin, rows, to in ((0, 64, 0), (80, 64, 64), (64, 16, 128)):
                pltpu.make_async_copy(
                    source.at[:, pl.ds(begin, rows), pl.ds(384 * n, 384)],
                    wbuf.at[n, :, pl.ds(to, rows), pl.ds(384 * half, 384)],
                    w_sem.at[n],
                ).start()

    odd = y % 2
    nt = (((1,), (1,)), ((), ()))

    def picks(shape, row_of, col_of):
        r = lax.broadcasted_iota(jnp.int32, shape, 0)
        c = lax.broadcasted_iota(jnp.int32, shape, 1)
        return jnp.where(row_of(r, c) & col_of(r, c), 1.0, 0.0).astype(BF16)

    def main_pick(to_high):
        return picks((72, 128), lambda r, c: (r - 8 * odd) == (c - 64 * to_high),
                     lambda r, c: (c - 64 * to_high >= 0) & (c - 64 * to_high < 64))

    def tail_pick(to_high):
        return picks((16, 72), lambda r, c: c == (r - 8 * to_high) + 64 * (1 - odd),
                     lambda r, c: (r - 8 * to_high >= 0) & (r - 8 * to_high < 8))

    main_top, main_bottom = main_pick(odd), main_pick(1 - odd)
    tail_top, tail_bottom = tail_pick(odd), tail_pick(1 - odd)

    def chunk_rows(c, half):
        def row_pick(columns, source_of):
            r = lax.broadcasted_iota(jnp.int32, (128, columns), 0)
            s = lax.broadcasted_iota(jnp.int32, (128, columns), 1)
            return jnp.where(source_of(r) == s, 1.0, 0.0).astype(BF16)

        if c < 2:
            pick = row_pick(512, lambda r: (r // 32) * 128 + 64 * half + 32 * c + r % 32)
            got = lax.dot_general(pick, prompt[...], nt, preferred_element_type=F32)
        else:
            got = 0.0
            for s in range(2):
                pick = row_pick(128, lambda r: jnp.where((r % 32) // 16 == s, (r // 32) * 32 + 16 * half + r % 16, -1))
                got += lax.dot_general(pick, decode[2 * (c - 2) + s], nt, preferred_element_type=F32)
        return got.astype(BF16)

    def pack(c):
        top, bottom = chunk_rows(c, 0), chunk_rows(c, 1)
        main = jnp.dot(top, main_top, preferred_element_type=F32)
        main += jnp.dot(bottom, main_bottom, preferred_element_type=F32)
        tail = lax.dot_general(tail_top, top, nt, preferred_element_type=F32)
        tail += lax.dot_general(tail_bottom, bottom, nt, preferred_element_type=F32)
        pieces[c, 0, y, 0:128, :] = main.astype(BF16)
        pieces[c, 0, y, 128:144, :] = tail.astype(BF16)

    def copy(c, name):
        slots, y_shift, rows, to_slots, hop = PLANS[c][name]
        rows = rows_of(c, rows)
        if y_shift is None:
            y_at = slice(None)
        elif y_shift in ("pairp", "pairm"):
            y_at = pl.ds(0 if y_shift == "pairp" else 2, 2)
        else:
            y_at = at_y(y_shift)

        def view(s):
            s = pl.ds(s[0], s[1] - s[0]) if isinstance(s, tuple) else s
            return pieces.at[c, s, y_at, rows, :]

        i = COPY_INDEX[c][name]
        return pltpu.make_async_remote_copy(
            src_ref=view(slots), dst_ref=view(to_slots), send_sem=ag_send.at[c, i], recv_sem=ag_recv.at[c, i],
            device_id=device(*hop), device_id_type=MESH)

    top_at = pl.multiple_of(core * 128, 128)
    bottom_at = pl.multiple_of((1 - core) * 128, 128)

    def unpack(c):
        low = lax.broadcasted_iota(jnp.int32, (128, 128), 1) < 64
        first = lax.broadcasted_iota(jnp.int32, (16, 128), 0) < 8
        def body(slot, carry):
            away = (slot + 1) // 2
            source = lax.rem(z + jnp.where(slot % 2 == 0, away, NZ - away), NZ)
            for yp in range(2):
                m = source * 2 + yp
                e = pieces[c, slot, 2 * yp, 0:128, :]
                o = pieces[c, slot, 2 * yp + 1, 0:128, :]
                lanes = pl.ds(pl.multiple_of(m * 128, 128), 128)
                xs[pl.ds(top_at, 128), lanes] = jnp.where(low, e, o)
                xs[pl.ds(bottom_at, 128), lanes] = pltpu.roll(jnp.where(low, o, e), 64, 1)
                te = pieces[c, slot, 2 * yp, 128:144, :].astype(F32)
                to = pieces[c, slot, 2 * yp + 1, 128:144, :].astype(F32)
                tails[m, :, pl.ds(top_at, 128)] = jnp.where(first, te, to)
                tails[m, :, pl.ds(bottom_at, 128)] = pltpu.roll(jnp.where(first, to, te), 8, 0)
            return carry

        lax.fori_loop(0, NZ, body, 0)
        xs[:, 2048:2304] = tails[...].reshape(256, 256).T.astype(BF16)

    def rs(g, name):
        i = ("pair", "far_down", "far_up", "down", "up", "across").index(name)
        if i == 0:
            src, dst, to = psend.at[g], precv.at[g], ("core", 1)
        elif i < 3:
            src, dst, to = s1_out.at[g, i - 1], s1_in.at[g, i - 1], ("x", (-1, 1)[i - 1])
        else:
            src, dst, to = s2_out.at[g, i - 3], s2_in.at[g, i - 3], ("x", (-1, 1, 2)[i - 3])
        return pltpu.make_async_remote_copy(
            src_ref=src, dst_ref=dst, send_sem=rs_send.at[g, i], recv_sem=rs_recv.at[g, i],
            device_id=device(*to), device_id_type=MESH)

    def multiply(g):
        n = lax.rem(g, THIRDS)

        @pl.when(g < THIRDS)
        def _():
            pltpu.make_async_copy(wbuf.at[n], wbuf.at[n], w_sem.at[n]).wait()

        @pl.when(n == 0)
        def _():
            unpack(g // THIRDS)

        acc = jnp.dot(xs[:, 0:2048], wbuf[n, :, 0:128, :].reshape(2048, 768), preferred_element_type=F32)
        acc += jnp.dot(xs[:, 2048:2304], wbuf[n, :, 128:144, :].reshape(256, 768), preferred_element_type=F32)
        psend[g] = acc[128:256].astype(BF16)
        rs(g, "pair").start()
        own[lax.rem(g, 6)] = acc[0:128]

    def block(shift):
        return pl.ds(pl.multiple_of(at_x(shift) * 32, 32), 32)

    def reduce_1(g):
        rs(g, "pair").wait_recv()

        def pair_sum(shift):
            rows = block(shift)
            return own[g % 6, rows, :] + precv[g, rows, :].astype(F32)

        if g in SHORT:
            for i, (name, shift) in enumerate((("down", -1), ("up", 1), ("across", 2))):
                s2_out[g, i] = pair_sum(shift).astype(BF16)
            for name in ("across", "down", "up"):
                rs(g, name).start()
        else:
            far = pair_sum(2).astype(BF16)
            s1_out[g, 0] = far[0:16]
            s1_out[g, 1] = far[16:32]
            rs(g, "far_down").start()
            rs(g, "far_up").start()
            for shift in (-1, 1):
                own[g % 6, block(shift), :] = pair_sum(shift)
        own[g % 6, block(0), :] = pair_sum(0)

    def reduce_2(g):
        rs(g, "far_down").wait_recv()
        rs(g, "far_up").wait_recv()
        below, above = own[g % 6, block(-1), :], own[g % 6, block(1), :]
        s2_out[g, 0, 0:16] = (below[0:16] + s1_in[g, 0].astype(F32)).astype(BF16)
        s2_out[g, 0, 16:32] = below[16:32].astype(BF16)
        rs(g, "down").start()
        s2_out[g, 1, 0:16] = above[0:16].astype(BF16)
        s2_out[g, 1, 16:32] = (above[16:32] + s1_in[g, 1].astype(F32)).astype(BF16)
        rs(g, "up").start()

    def reduce_3(g):
        c, n = g // THIRDS, g % THIRDS
        rs(g, "down").wait_recv()
        rs(g, "up").wait_recv()
        total = own[g % 6, block(0), :] + s2_in[g, 0].astype(F32) + s2_in[g, 1].astype(F32)
        if g in SHORT:
            rs(g, "across").wait_recv()
            total += s2_in[g, 2].astype(F32)
        hidden = (jax.nn.silu(total[:, 0:384]) * total[:, 384:768]).astype(BF16)
        columns = pl.ds(384 * n, 384)
        if c < 2:
            out[0, pl.ds(32 * c, 32), columns] = hidden
        else:
            out[1, pl.ds(32 * (c - 2), 32), columns] = hidden

    arrived = set()

    def perform(kind, number, index):
        if kind in ("R1", "R2", "R3"):
            {"R1": reduce_1, "R2": reduce_2, "R3": reduce_3}[kind](number)
            return
        before, after = STEPS[number][kind, index]
        if kind == "pack":
            pack(number)
        for name in before:
            if (number, name) not in arrived:
                copy(number, name).wait_recv()
                arrived.add((number, name))
        for name in after:
            copy(number, name).start()

    between = [[]]
    for kind, number, index in ORDER:
        if kind == "MM":
            between.append([])
        else:
            between[-1].append((kind, number, index))
    pack(0)
    pl.semaphore_wait(barrier, len(hops))
    for name in STEPS[0]["pack", 0][1]:
        copy(0, name).start()
    between[0].remove(("pack", 0, 0))
    for work in between[0]:
        perform(*work)

    def round_of(g, carry):
        multiply(g)

        def follow(lo, hi):
            if hi - lo == 1:
                for work in between[lo + 1]:
                    perform(*work)
                return
            middle = (lo + hi) // 2

            @pl.when(g < middle)
            def _():
                follow(lo, middle)

            @pl.when(g >= middle)
            def _():
                follow(middle, hi)

        follow(0, GROUPS)
        return carry

    lax.fori_loop(0, GROUPS, round_of, 0)
    for c in range(CHUNKS):
        for name in PLANS[c]:
            assert (c, name) in arrived
            copy(c, name).wait_send()
    for g in range(GROUPS):
        for name in ("pair", "down", "up") + (("across",) if g in SHORT else ("far_down", "far_up")):
            rs(g, name).wait_send()


def shards(prompt_tokens, decode_tokens, gate_weight, up_weight):
    gate_weight = gate_weight.reshape(16, 144, 1152)
    up_weight = up_weight.reshape(16, 144, 1152)
    vmem = pl.BlockSpec(memory_space=pltpu.VMEM)
    anywhere = pl.BlockSpec(memory_space=pl.ANY)
    both = pl.pallas_call(
        kernel,
        out_shape=jax.ShapeDtypeStruct((2, 64, 1152), BF16),
        in_specs=[vmem, vmem, anywhere, anywhere],
        out_specs=vmem,
        scratch_shapes=[
            pltpu.VMEM((CHUNKS, NZ, NY, 144, 128), BF16),
            pltpu.VMEM((THIRDS, 16, 144, 768), BF16),
            pltpu.VMEM((256, 2304), BF16),
            pltpu.VMEM((16, 16, 256), F32),
            pltpu.VMEM((6, 128, 768), F32),
            pltpu.VMEM((GROUPS, 128, 768), BF16),
            pltpu.VMEM((GROUPS, 128, 768), BF16),
            pltpu.VMEM((GROUPS, 2, 16, 768), BF16),
            pltpu.VMEM((GROUPS, 2, 16, 768), BF16),
            pltpu.VMEM((GROUPS, 3, 32, 768), BF16),
            pltpu.VMEM((GROUPS, 3, 32, 768), BF16),
            pltpu.SemaphoreType.DMA((CHUNKS, MOST)),
            pltpu.SemaphoreType.DMA((CHUNKS, MOST)),
            pltpu.SemaphoreType.DMA((GROUPS, 6)),
            pltpu.SemaphoreType.DMA((GROUPS, 6)),
            pltpu.SemaphoreType.DMA((THIRDS,)),
        ],
        compiler_params=pltpu.CompilerParams(
            collective_id=0, has_side_effects=True, vmem_limit_bytes=56 * 1024 * 1024),
        cost_estimate=pl.CostEstimate(flops=2 * 1024 * 2304 * 2304, bytes_accessed=11_000_000, transcendentals=147456),
    )(prompt_tokens.T, decode_tokens.transpose(0, 2, 1), gate_weight, up_weight)
    return both[0], both[1].reshape(4, 16, 1152)


def solution(mesh):
    in_specs = (P(None, ("gx", "gy")), P(None, None, ("gx", "gy")), P("gx", "gy"), P("gx", "gy"))
    out_specs = (P("gx", "gy"), P(None, "gx", "gy"))
    return jax.shard_map(shards, mesh=mesh, in_specs=in_specs, out_specs=out_specs, check_vma=False)
```

```python
import functools

import jax
import jax.numpy as jnp
from jax import lax
from jax.experimental import pallas as pl
from jax.experimental.pallas import tpu as pltpu
from jax.sharding import PartitionSpec as P

MESH = pl.DeviceIdType.MESH
NX, NZ, NY = 4, 8, 4
CHUNKS, THIRDS = 4, 3
GROUPS = CHUNKS * THIRDS
BF16, F32 = jnp.bfloat16, jnp.float32

SPLIT = (32, 64, 48, 48)
STRAIGHT = (True, True, False, False)
SETS = (((0, 5), (5, 8)), ((0, 5), (5, 8)), ((0, 5), (5, 8)), ((0, 3), (3, 5), (5, 8)))
WIDE = (False, False, False, False)
LEAP = (False, False, False, False)
SHORT = (8, 9, 10, 11)
ORDER = (
    ("pack", 0, 0), ("A1", 0, 0), ("pack", 1, 0), ("pack", 2, 0), ("Y", 0, 0), ("A2", 0, 0), ("Y", 0, 1),
    ("A1", 1, 0), ("Y", 1, 0), ("A1", 2, 0), ("pack", 3, 0), ("E", 0, 0), ("B1", 2, 0), ("A3", 0, 0), ("E", 0, 1),
    ("A2", 1, 0), ("Y", 1, 1), ("A2", 2, 0), ("B2", 2, 0), ("E", 1, 0), ("A1", 3, 0), ("Y", 2, 0), ("B1", 3, 0),
    ("U", 0, 0), ("A3", 1, 0), ("MM", 0, 0), ("E", 1, 1), ("MM", 1, 0), ("Y", 2, 1), ("A3", 2, 0), ("R1", 0, 0),
    ("MM", 2, 0), ("R1", 1, 0), ("E", 2, 0), ("A2", 3, 0), ("B2", 3, 0), ("Y", 3, 0), ("R1", 2, 0), ("U", 1, 0),
    ("R2", 0, 0), ("Y", 3, 1), ("MM", 3, 0), ("R2", 1, 0), ("E", 2, 1), ("MM", 4, 0), ("R2", 2, 0), ("R1", 3, 0),
    ("A3", 3, 0), ("Y", 3, 2), ("MM", 5, 0), ("R1", 4, 0), ("E", 3, 0), ("R3", 0, 0), ("U", 2, 0), ("E", 3, 1),
    ("R1", 5, 0), ("R3", 1, 0), ("MM", 6, 0), ("R2", 3, 0), ("R3", 2, 0), ("E", 3, 2), ("MM", 7, 0), ("R2", 4, 0),
    ("R1", 6, 0), ("MM", 8, 0), ("R2", 5, 0), ("R1", 7, 0), ("U", 3, 0), ("R1", 8, 0), ("R3", 3, 0), ("MM", 9, 0),
    ("R2", 6, 0), ("R3", 4, 0), ("MM", 10, 0), ("R2", 7, 0), ("R1", 9, 0), ("R3", 5, 0), ("MM", 11, 0),
    ("R1", 10, 0), ("R3", 6, 0), ("R1", 11, 0), ("R3", 7, 0), ("R3", 8, 0), ("R3", 9, 0), ("R3", 10, 0),
    ("R3", 11, 0),
)

SLOT = {0: 0, -1: 1, 1: 2, -2: 3, 2: 4, -3: 5, 3: 6, 4: 7, -4: 7}
DISTANCE = (0, 1, 1, 2, 2, 3, 3, 4)


def rows_of(c, which):
    split = SPLIT[c]
    half = {96: 48, 80: 48, 112: 64, 128: 64}[144 - split]
    begin, size = {"a": (0, split), "b": (split, 144 - split), "low": (split, half), "high": (split + half, 144 - split - half)}[which]
    return pl.ds(begin, size)


def plan(c):
    copies = {"a1p": (0, 0, "a", 0, ("y", 1)), "a1m": (0, 0, "a", 0, ("y", -1)), "a1x": (0, 0, "a", 0, ("y", 2))}
    for s, way in ((1, "p"), (-1, "m")):
        for d in (1, 2, 3):
            leap = 2 if d == 2 and LEAP[c] else 1
            copies[f"c{d}{way}"] = (SLOT[-s * (d - leap)], None, "a", SLOT[-s * d], ("z", s * leap))
        copies[f"c4{way}"] = (SLOT[-2 * s], "pair" + way, "a", 7, ("z", 2 * s))
        if STRAIGHT[c]:
            for d in (1, 2, 3):
                copies[f"b{d}{way}"] = (0, 0, "b", SLOT[-s * d], ("z", s * d))
        else:
            for d in (1, 2, 3):
                copies[f"b{d}{way}"] = (SLOT[-s * (d - 1)], 0, "b", SLOT[-s * d], ("z", s))
            copies[f"b4{way}"] = (SLOT[-2 * s], 0, "low" if s > 0 else "high", 7, ("z", 2 * s))
        for i, (lo, hi) in enumerate(SETS[c]):
            copies[f"d{i}{way}"] = ((lo, hi), 0, "b", (lo, hi), ("y", s))
            if WIDE[c]:
                copies[f"x{i}"] = ((lo, hi), 0, "b", (lo, hi), ("y", 2))
            else:
                copies[f"e{i}{way}"] = ((lo, hi), -s, "low" if s > 0 else "high", (lo, hi), ("y", s))
    if STRAIGHT[c]:
        copies["b4"] = (0, 0, "b", 7, ("z", 4))
    return copies


PLANS = [plan(c) for c in range(CHUNKS)]
COPY_INDEX = [{name: i for i, name in enumerate(p)} for p in PLANS]
MOST = max(len(p) for p in PLANS)


def steps(c):
    straight = STRAIGHT[c]
    table = {
        ("A1", 0): (("a1p", "a1m", "a1x"), ("c1p", "c1m")),
        ("A2", 0): (("c1p", "c1m"), ("c2p", "c2m")),
        ("A3", 0): (("c2p", "c2m"), ("c4p", "c4m", "c3p", "c3m")),
    }
    if LEAP[c]:
        table["A1", 0] = (("a1p", "a1m", "a1x"), ("c2p", "c2m", "c1p", "c1m"))
        del table["A2", 0]
    first = ["a1p", "a1m", "a1x"]
    if straight:
        first += ["b1p", "b1m", "b2p", "b2m", "b3p", "b3m", "b4"]
    else:
        first += ["b1p", "b1m"]
        table["B1", 0] = (("b1p", "b1m"), ("b2p", "b2m"))
        table["B2", 0] = (("b2p", "b2m"), ("b4p", "b4m", "b3p", "b3m"))
    table["pack", 0] = ((), tuple(first))
    done = ["c1p", "c1m", "c3p", "c3m", "c4p", "c4m"]
    for i, (lo, hi) in enumerate(SETS[c]):
        need = []
        for d in sorted(set(DISTANCE[lo:hi])):
            need += {0: [], 4: ["b4"] if straight else ["b4p", "b4m"]}.get(d, [f"b{d}p", f"b{d}m"])
        if WIDE[c]:
            table["Y", i] = (tuple(need), (f"x{i}", f"d{i}p", f"d{i}m"))
            done += [f"d{i}p", f"d{i}m", f"x{i}"]
        else:
            table["Y", i] = (tuple(need), (f"d{i}p", f"d{i}m"))
            table["E", i] = ((f"d{i}p", f"d{i}m"), (f"e{i}p", f"e{i}m"))
            done += [f"e{i}p", f"e{i}m"]
    table["U", 0] = (tuple(done), ())
    return table


STEPS = [steps(c) for c in range(CHUNKS)]


def kernel(prompt, decode, gate, up, out, pieces, wbuf, xs, tails, own, psend, precv,
           s1_out, s1_in, s2_out, s2_in, ag_send, ag_recv, rs_send, rs_recv, w_sem):
    gx, gy = lax.axis_index("gx"), lax.axis_index("gy")
    x, core = gx // 2, gx % 2
    z, y = gy // NY, gy % NY

    def at_y(shift):
        return lax.rem(y + (shift + NY), NY)

    def at_x(shift):
        return lax.rem(x + (shift + NX), NX)

    def device(axis, shift):
        if axis == "core":
            return {"gx": x * 2 + (1 - core), "gy": gy}
        if axis == "x":
            return {"gx": at_x(shift) * 2 + core, "gy": gy}
        if axis == "y":
            return {"gx": gx, "gy": z * NY + at_y(shift)}
        return {"gx": gx, "gy": lax.rem(z + (shift + NZ), NZ) * NY + y}

    barrier = pltpu.get_barrier_semaphore()
    hops = {("core", 1), ("x", 1), ("x", -1)} | {p[name][4] for p in PLANS for name in p}
    if SHORT:
        hops.add(("x", 2))
    for axis, shift in sorted(hops):
        pl.semaphore_signal(barrier, inc=1, device_id=device(axis, shift), device_id_type=MESH)

    odd = y % 2
    nt = (((1,), (1,)), ((), ()))

    def picks(shape, row_of, col_of):
        r = lax.broadcasted_iota(jnp.int32, shape, 0)
        c = lax.broadcasted_iota(jnp.int32, shape, 1)
        return jnp.where(row_of(r, c) & col_of(r, c), 1.0, 0.0).astype(BF16)

    def main_pick(to_high):
        return picks((72, 128), lambda r, c: (r - 8 * odd) == (c - 64 * to_high),
                     lambda r, c: (c - 64 * to_high >= 0) & (c - 64 * to_high < 64))

    def tail_pick(to_high):
        return picks((16, 72), lambda r, c: c == (r - 8 * to_high) + 64 * (1 - odd),
                     lambda r, c: (r - 8 * to_high >= 0) & (r - 8 * to_high < 8))

    main_top, main_bottom = main_pick(odd), main_pick(1 - odd)
    tail_top, tail_bottom = tail_pick(odd), tail_pick(1 - odd)

    def chunk_rows(c, half):
        def row_pick(columns, source_of):
            r = lax.broadcasted_iota(jnp.int32, (128, columns), 0)
            s = lax.broadcasted_iota(jnp.int32, (128, columns), 1)
            return jnp.where(source_of(r) == s, 1.0, 0.0).astype(BF16)

        if c < 2:
            pick = row_pick(512, lambda r: (r // 32) * 128 + 64 * half + 32 * c + r % 32)
            got = lax.dot_general(pick, prompt[...], nt, preferred_element_type=F32)
        else:
            got = 0.0
            for s in range(2):
                pick = row_pick(128, lambda r: jnp.where((r % 32) // 16 == s, (r // 32) * 32 + 16 * half + r % 16, -1))
                got += lax.dot_general(pick, decode[2 * (c - 2) + s], nt, preferred_element_type=F32)
        return got.astype(BF16)

    def pack(c):
        top, bottom = chunk_rows(c, 0), chunk_rows(c, 1)
        main = jnp.dot(top, main_top, preferred_element_type=F32)
        main += jnp.dot(bottom, main_bottom, preferred_element_type=F32)
        tail = lax.dot_general(tail_top, top, nt, preferred_element_type=F32)
        tail += lax.dot_general(tail_bottom, bottom, nt, preferred_element_type=F32)
        pieces[c, 0, y, 0:128, :] = main.astype(BF16)
        pieces[c, 0, y, 128:144, :] = tail.astype(BF16)

    def copy(c, name):
        slots, y_shift, rows, to_slots, hop = PLANS[c][name]
        rows = rows_of(c, rows)
        if y_shift is None:
            y_at = slice(None)
        elif y_shift in ("pairp", "pairm"):
            y_at = pl.ds(0 if y_shift == "pairp" else 2, 2)
        else:
            y_at = at_y(y_shift)

        def view(s):
            s = pl.ds(s[0], s[1] - s[0]) if isinstance(s, tuple) else s
            return pieces.at[c, s, y_at, rows, :]

        i = COPY_INDEX[c][name]
        return pltpu.make_async_remote_copy(
            src_ref=view(slots), dst_ref=view(to_slots), send_sem=ag_send.at[c, i], recv_sem=ag_recv.at[c, i],
            device_id=device(*hop), device_id_type=MESH)

    top_at = pl.multiple_of(core * 128, 128)
    bottom_at = pl.multiple_of((1 - core) * 128, 128)

    def unpack(c):
        low = lax.broadcasted_iota(jnp.int32, (128, 128), 1) < 64
        first = lax.broadcasted_iota(jnp.int32, (16, 128), 0) < 8
        def body(slot, carry):
            away = (slot + 1) // 2
            source = lax.rem(z + jnp.where(slot % 2 == 0, away, NZ - away), NZ)
            for yp in range(2):
                m = source * 2 + yp
                e = pieces[c, slot, 2 * yp, 0:128, :]
                o = pieces[c, slot, 2 * yp + 1, 0:128, :]
                lanes = pl.ds(pl.multiple_of(m * 128, 128), 128)
                xs[pl.ds(top_at, 128), lanes] = jnp.where(low, e, o)
                xs[pl.ds(bottom_at, 128), lanes] = pltpu.roll(jnp.where(low, o, e), 64, 1)
                te = pieces[c, slot, 2 * yp, 128:144, :].astype(F32)
                to = pieces[c, slot, 2 * yp + 1, 128:144, :].astype(F32)
                tails[m, :, pl.ds(top_at, 128)] = jnp.where(first, te, to)
                tails[m, :, pl.ds(bottom_at, 128)] = pltpu.roll(jnp.where(first, to, te), 8, 0)
            return carry

        lax.fori_loop(0, NZ, body, 0)
        xs[:, 2048:2304] = tails[...].reshape(256, 256).T.astype(BF16)

    def rs(g, name):
        i = ("pair", "far_down", "far_up", "down", "up", "across").index(name)
        if i == 0:
            src, dst, to = psend.at[g], precv.at[g], ("core", 1)
        elif i < 3:
            src, dst, to = s1_out.at[g, i - 1], s1_in.at[g, i - 1], ("x", (-1, 1)[i - 1])
        else:
            src, dst, to = s2_out.at[g, i - 3], s2_in.at[g, i - 3], ("x", (-1, 1, 2)[i - 3])
        return pltpu.make_async_remote_copy(
            src_ref=src, dst_ref=dst, send_sem=rs_send.at[g, i], recv_sem=rs_recv.at[g, i],
            device_id=device(*to), device_id_type=MESH)

    def multiply(g):
        n = lax.rem(g, THIRDS)

        @pl.when(g < THIRDS)
        def _():
            pltpu.make_async_copy(wbuf.at[n], wbuf.at[n], w_sem.at[n]).wait()

        @pl.when(n == 0)
        def _():
            unpack(g // THIRDS)

        weights = jnp.concatenate(
            [wbuf[n, :, 0:128, :].reshape(2048, 768), wbuf[n, :, 128:144, :].reshape(256, 768)], axis=0)
        acc = jnp.dot(xs[...], weights, preferred_element_type=F32)
        psend[g] = acc[128:256].astype(BF16)
        rs(g, "pair").start()
        own[lax.rem(g, 6)] = acc[0:128]

    def block(shift):
        return pl.ds(pl.multiple_of(at_x(shift) * 32, 32), 32)

    def reduce_1(g):
        rs(g, "pair").wait_recv()

        def pair_sum(shift):
            rows = block(shift)
            return own[g % 6, rows, :] + precv[g, rows, :].astype(F32)

        if g in SHORT:
            for i, (name, shift) in enumerate((("down", -1), ("up", 1), ("across", 2))):
                s2_out[g, i] = pair_sum(shift).astype(BF16)
            for name in ("across", "down", "up"):
                rs(g, name).start()
        else:
            far = pair_sum(2).astype(BF16)
            s1_out[g, 0] = far[0:16]
            s1_out[g, 1] = far[16:32]
            rs(g, "far_down").start()
            rs(g, "far_up").start()
            for shift in (-1, 1):
                own[g % 6, block(shift), :] = pair_sum(shift)
        own[g % 6, block(0), :] = pair_sum(0)

    def reduce_2(g):
        rs(g, "far_down").wait_recv()
        rs(g, "far_up").wait_recv()
        below, above = own[g % 6, block(-1), :], own[g % 6, block(1), :]
        s2_out[g, 0, 0:16] = (below[0:16] + s1_in[g, 0].astype(F32)).astype(BF16)
        s2_out[g, 0, 16:32] = below[16:32].astype(BF16)
        rs(g, "down").start()
        s2_out[g, 1, 0:16] = above[0:16].astype(BF16)
        s2_out[g, 1, 16:32] = (above[16:32] + s1_in[g, 1].astype(F32)).astype(BF16)
        rs(g, "up").start()

    def reduce_3(g):
        c, n = g // THIRDS, g % THIRDS
        rs(g, "down").wait_recv()
        rs(g, "up").wait_recv()
        total = own[g % 6, block(0), :] + s2_in[g, 0].astype(F32) + s2_in[g, 1].astype(F32)
        if g in SHORT:
            rs(g, "across").wait_recv()
            total += s2_in[g, 2].astype(F32)
        hidden = (jax.nn.silu(total[:, 0:384]) * total[:, 384:768]).astype(BF16)
        columns = pl.ds(384 * n, 384)
        if c < 2:
            out[0, pl.ds(32 * c, 32), columns] = hidden
        else:
            out[1, pl.ds(32 * (c - 2), 32), columns] = hidden

    arrived = set()

    def perform(kind, number, index):
        if kind in ("R1", "R2", "R3"):
            {"R1": reduce_1, "R2": reduce_2, "R3": reduce_3}[kind](number)
            return
        before, after = STEPS[number][kind, index]
        if kind == "pack":
            pack(number)
        for name in before:
            if (number, name) not in arrived:
                copy(number, name).wait_recv()
                arrived.add((number, name))
        for name in after:
            copy(number, name).start()

    between = [[]]
    for kind, number, index in ORDER:
        if kind == "MM":
            between.append([])
        else:
            between[-1].append((kind, number, index))
    pack(0)
    pl.semaphore_wait(barrier, len(hops))
    for name in STEPS[0]["pack", 0][1]:
        copy(0, name).start()

    for n in range(THIRDS):
        for half, source in enumerate((gate, up)):
            for begin, rows, to in ((0, 64, 0), (80, 64, 64), (64, 16, 128)):
                pltpu.make_async_copy(
                    source.at[:, pl.ds(begin, rows), pl.ds(384 * n, 384)],
                    wbuf.at[n, :, pl.ds(to, rows), pl.ds(384 * half, 384)],
                    w_sem.at[n],
                ).start()

    between[0].remove(("pack", 0, 0))
    for work in between[0]:
        perform(*work)

    def round_of(g, carry):
        multiply(g)

        def follow(lo, hi):
            if hi - lo == 1:
                for work in between[lo + 1]:
                    perform(*work)
                return
            middle = (lo + hi) // 2

            @pl.when(g < middle)
            def _():
                follow(lo, middle)

            @pl.when(g >= middle)
            def _():
                follow(middle, hi)

        follow(0, GROUPS)
        return carry

    lax.fori_loop(0, GROUPS, round_of, 0)
    for c in range(CHUNKS):
        for name in PLANS[c]:
            assert (c, name) in arrived
            copy(c, name).wait_send()
    for g in range(GROUPS):
        for name in ("pair", "down", "up") + (("across",) if g in SHORT else ("far_down", "far_up")):
            rs(g, name).wait_send()


def shards(prompt_tokens, decode_tokens, gate_weight, up_weight):
    gate_weight = gate_weight.reshape(16, 144, 1152)
    up_weight = up_weight.reshape(16, 144, 1152)
    vmem = pl.BlockSpec(memory_space=pltpu.VMEM)
    anywhere = pl.BlockSpec(memory_space=pl.ANY)
    both = pl.pallas_call(
        kernel,
        out_shape=jax.ShapeDtypeStruct((2, 64, 1152), BF16),
        in_specs=[vmem, vmem, anywhere, anywhere],
        out_specs=vmem,
        scratch_shapes=[
            pltpu.VMEM((CHUNKS, NZ, NY, 144, 128), BF16),
            pltpu.VMEM((THIRDS, 16, 144, 768), BF16),
            pltpu.VMEM((256, 2304), BF16),
            pltpu.VMEM((16, 16, 256), F32),
            pltpu.VMEM((6, 128, 768), F32),
            pltpu.VMEM((GROUPS, 128, 768), BF16),
            pltpu.VMEM((GROUPS, 128, 768), BF16),
            pltpu.VMEM((GROUPS, 2, 16, 768), BF16),
            pltpu.VMEM((GROUPS, 2, 16, 768), BF16),
            pltpu.VMEM((GROUPS, 3, 32, 768), BF16),
            pltpu.VMEM((GROUPS, 3, 32, 768), BF16),
            pltpu.SemaphoreType.DMA((CHUNKS, MOST)),
            pltpu.SemaphoreType.DMA((CHUNKS, MOST)),
            pltpu.SemaphoreType.DMA((GROUPS, 6)),
            pltpu.SemaphoreType.DMA((GROUPS, 6)),
            pltpu.SemaphoreType.DMA((THIRDS,)),
        ],
        compiler_params=pltpu.CompilerParams(
            collective_id=0, has_side_effects=True, vmem_limit_bytes=56 * 1024 * 1024),
        cost_estimate=pl.CostEstimate(flops=2 * 1024 * 2304 * 2304, bytes_accessed=11_000_000, transcendentals=147456),
    )(prompt_tokens.T, decode_tokens.transpose(0, 2, 1), gate_weight, up_weight)
    return both[0], both[1].reshape(4, 16, 1152)


def solution(mesh):
    in_specs = (P(None, ("gx", "gy")), P(None, None, ("gx", "gy")), P("gx", "gy"), P("gx", "gy"))
    out_specs = (P("gx", "gy"), P(None, "gx", "gy"))
    return jax.shard_map(shards, mesh=mesh, in_specs=in_specs, out_specs=out_specs, check_vma=False)
```
